32 devices in a mesh: groups: 2 (over y), replica: 4 (over z), tensor: 4 (over x, core).
Axes of the slice: x: 2, y: 2, z: 4, core: 2. Of those that a mesh axis runs over, the one named last changes fastest.
Arguments:
- holder: int32 [88, 1], P('groups'), parts along dimension 0, may hold values from 0 to 3; in each aligned block of 11 rows (0 to 10, 11 to 21, ...) at most 3 rows name the same one
- cache_slot: int32 [88], P('groups'), parts along dimension 0, may hold values from 0 to 5
- prefix_pages: int32 [88], P(('groups', 'replica')), parts along dimension 0, may hold values from 1 to 8, as said below
- page_ids: int32 [88, 8], P('groups'), parts along dimension 0, may hold values from 0 to 47
- suffix_length: int32 [88], P(('groups', 'replica')), parts along dimension 0, may hold values from 2 to 32, as said below
- cache_states: bfloat16 [48, 128, 64, 128], P(('groups', 'replica'), 'tensor'), parts along dimension 0, may hold values from -0.59765625 to 0.59765625
- page_keys: bfloat16 [384, 16, 1024], P(('groups', 'replica'), None, 'tensor'), parts along dimension 0, may hold values from -5 to 5
- page_values: bfloat16 [384, 16, 1024], P(('groups', 'replica'), None, 'tensor'), parts along dimension 0, may hold values from -5 to 5
- ssm_inputs: bfloat16 [88, 32, 8192], P(('groups', 'replica'), None, 'tensor'), parts along dimension 0, may hold values from -6 to 6
- step_sizes: float32 [88, 32, 128], P(('groups', 'replica'), None, 'tensor'), parts along dimension 0, may hold values from 0.0002 to 0.7
- log_rates: float32 [128], P('tensor'), may hold values from -0.5 to 0.5
- write_map: bfloat16 [88, 32, 512], P(('groups', 'replica'), None, 'tensor'), parts along dimension 0, may hold values from -6 to 6
- read_map: bfloat16 [88, 32, 512], P(('groups', 'replica'), None, 'tensor'), parts along dimension 0, may hold values from -6 to 6
- skip_gain: float32 [128], P('tensor'), may hold values from 0.5 to 1.5
- gate_values: bfloat16 [88, 32, 8192], P(('groups', 'replica'), None, 'tensor'), parts along dimension 0, may hold values from -8 to 8
- norm_gain: float32 [8192], P('tensor'), may hold values from 0.25 to 1.75
- queries: bfloat16 [88, 32, 8192], P(('groups', 'replica'), None, 'tensor'), parts along dimension 0, may hold values from -8 to 8
- suffix_keys: bfloat16 [88, 32, 1024], P(('groups', 'replica'), None, 'tensor'), parts along dimension 0, may hold values from -8 to 8
- suffix_values: bfloat16 [88, 32, 1024], P(('groups', 'replica'), None, 'tensor'), parts along dimension 0, may hold values from -5 to 5
Outputs:
- mamba_output: bfloat16 [88, 32, 8192], P(('groups', 'replica'), None, 'tensor'), parts along dimension 0
- attention_output: bfloat16 [88, 32, 8192], P(('groups', 'replica'), None, 'tensor'), parts along dimension 0
The draws below stay inside these ranges and needn't reach their ends.
There are 2 independent parts, one for each index of `groups`. The reference program is written for one: setup_inputs(seed, part) draws one part's arguments, and reference() takes and returns one part's arrays. A program takes and returns all parts, laid end to end along the dimension named above; an argument that names none is the same for every part. Nothing has to cross between parts.
Inputs may be any that keep to these rules, and one draw needn't show every extreme that they name: Within each replica's block of 11 requests no holder appears more than 3 times, and some holder appears exactly 3 times. `prefix_pages`: some request has 8 pages. `suffix_length`: some request has 32 live positions.
All inputs are finite; a program needn't handle non-finite values.
Results may differ from the reference program's by a relative error of at most 0.0051.
Values may be sent and summed in bfloat16 or wider, within the bound.
No kernel may reach another device: no remote copies, remote signals or barrier semaphores. Data moves between devices by JAX's collectives and lax.ppermute only.
A program may use at most 128 MiB of HBM per device.

```python
import math
import jax
import jax.numpy as jnp
import numpy as np
from jax import lax

SSM_HEADS = 128
SSM_HDIM = 64
STATE = 128
GROUPS = 4
Q_HEADS = 64
KV_HEADS = 8
HEAD_DIM = 128
TAIL_SPOTS = 32
PAGE = 16
MAXP = 8
REQ_DEV = 11
SLOTS = 6
POOL = 48
PAIR = 3
QUERY_COUNT_ALL = 44
CACHED = 24
PAGES_ALL = 192
N_REPLICA = 4


def draw_prefix_pages(key, part):
    key = jax.random.fold_in(key, 1)
    counts = jax.random.randint(key, (QUERY_COUNT_ALL,), 1, MAXP + 1)
    return jnp.where(jnp.arange(QUERY_COUNT_ALL) == 0, MAXP, counts).astype(jnp.int32)


def draw_suffix_length(key, part):
    key = jax.random.fold_in(key, 2)
    counts = jax.random.randint(key, (QUERY_COUNT_ALL,), 2, TAIL_SPOTS + 1)
    return jnp.where(jnp.arange(QUERY_COUNT_ALL) == 0, TAIL_SPOTS, counts).astype(jnp.int32)


def draw_step_sizes(key, part):
    key = jax.random.fold_in(key, 31)
    derived_seeds = jax.random.split(key, 7)
    fast_share = 0.5
    forgetful = jax.random.bernoulli(derived_seeds[0], fast_share, (SSM_HEADS,))
    fast_rate = jnp.exp(jax.random.uniform(derived_seeds[1], (SSM_HEADS,), minval=math.log(0.02), maxval=math.log(0.05)))
    slow_rate = jnp.exp(jax.random.uniform(derived_seeds[2], (SSM_HEADS,), minval=math.log(0.0008), maxval=math.log(0.003)))
    default_intensity = jnp.where(forgetful, fast_rate, slow_rate)
    query_multiplier_spread = jnp.exp(jax.random.uniform(derived_seeds[3], (QUERY_COUNT_ALL, 1, 1), minval=math.log(0.6), maxval=math.log(1.6)))
    element_multiplier_spread = jnp.exp(jax.random.uniform(derived_seeds[4], (QUERY_COUNT_ALL, TAIL_SPOTS, SSM_HEADS), minval=math.log(0.5), maxval=math.log(2.0)))
    spike_start = jax.random.randint(derived_seeds[5], (QUERY_COUNT_ALL, 2), 0, TAIL_SPOTS)
    spike_affected = jnp.any(jnp.arange(TAIL_SPOTS)[None, :, None] == spike_start[:, None, :], axis=-1)
    spike_span = jax.random.uniform(derived_seeds[6], (QUERY_COUNT_ALL, TAIL_SPOTS, 1), minval=0.25, maxval=0.5)
    extent_sequence = default_intensity[None, None, :] * query_multiplier_spread * element_multiplier_spread + jnp.where(spike_affected[:, :, None], spike_span, 0.0)
    return extent_sequence.astype(jnp.float32)


def draw_gate_values(key, part):
    key = jax.random.fold_in(key, 41)
    derived_seeds = jax.random.split(key, 3)
    row_width = SSM_HEADS * SSM_HDIM
    sample = jax.random.normal(derived_seeds[0], (QUERY_COUNT_ALL, TAIL_SPOTS, row_width))
    spread = 1.15
    column_scale = jnp.exp(jax.random.uniform(derived_seeds[1], (row_width,), minval=-spread, maxval=spread))
    row_scale = jnp.exp(jax.random.uniform(derived_seeds[2], (QUERY_COUNT_ALL, TAIL_SPOTS, 1), minval=-spread, maxval=spread))
    return jnp.clip(sample * column_scale[None, None, :] * row_scale, -8.0, 8.0).astype(jnp.bfloat16)


def draw_queries(key, part):
    key = jax.random.fold_in(key, 21)
    sample = jnp.clip(jax.random.normal(key, (QUERY_COUNT_ALL, TAIL_SPOTS, Q_HEADS * HEAD_DIM)), -5.0, 5.0)
    return sample.astype(jnp.bfloat16)


def draw_suffix_keys(key, part):
    key = jax.random.fold_in(key, 22)
    sample = jnp.clip(jax.random.normal(key, (QUERY_COUNT_ALL, TAIL_SPOTS, KV_HEADS * HEAD_DIM)), -5.0, 5.0)
    return sample.astype(jnp.bfloat16)


def with_ends(array, own_key, smallest, top_value):
    place = [jax.random.randint(jax.random.fold_in(own_key, axis), (), 0, length) for axis, length in enumerate(array.shape)]
    main_axis = array.shape.index(max(array.shape))
    next_to = place[:main_axis] + [(place[main_axis] + 1) % array.shape[main_axis]] + place[main_axis + 1:]
    return array.at[tuple(place)].set(smallest).at[tuple(next_to)].set(top_value)


def steps_of(rng, shape, shards, low, high):
    def one(dim, shards_of):
        heights = jax.random.uniform(jax.random.fold_in(jax.random.fold_in(rng, 6), dim), (shards_of,), jnp.float32, low / len(shards), high / len(shards))
        return jnp.repeat(jnp.exp(heights), shape[dim] // shards_of).reshape((-1,) + (1,) * (len(shape) - dim - 1))

    gain = one(*shards[0])
    for cut in shards[1:]:
        gain = gain * one(*cut)
    return gain


def routed_block(stream_key, own, number, rows, amount, top, most, slope):
    sequence = jax.random.permutation(stream_key, amount)
    crowded, usual = shares(amount, rows * top, most, slope, True), shares(amount, rows * top, most, slope, False)
    places = jnp.arange(amount)

    def named(lengths, rotation):
        used = int((lengths > 0).sum())
        fixed = max(1, used // 4)
        passed = fixed + (places - fixed + rotation * (used - fixed)) % max(1, amount - fixed)
        return jnp.zeros((amount,), jnp.int32).at[sequence[jnp.where(places < fixed, places, passed)]].set(jnp.asarray(lengths, jnp.int32))

    lengths = jnp.where(number % 4 == 0, named(crowded, number // 4), named(usual, number - number // 4 - 1))
    mixed = jax.random.permutation(jax.random.fold_in(own, 3), amount)
    giver, sink = mixed[0:amount // 2 * 2:2], mixed[1:amount // 2 * 2:2]
    margin = jnp.minimum(lengths[giver] - 1, most - lengths[sink]) // 2
    margin = jnp.where((giver == sequence[0]) | (sink == sequence[0]) | (lengths[sink] == 0), 0, jnp.maximum(margin, 0))
    passed = jax.random.randint(jax.random.fold_in(own, 4), (amount // 2,), 0, 1 << 20) % (margin + 1)
    lengths = lengths.at[giver].add(-passed).at[sink].add(passed)
    items = jnp.searchsorted(jnp.cumsum(lengths), jnp.arange(rows * top), side="right").astype(jnp.int32)
    listing = items.reshape(top, rows).T
    listing = listing[jax.random.permutation(jax.random.fold_in(own, 1), rows)]
    rotation = jax.random.randint(jax.random.fold_in(own, 2), (rows, 1), 0, top)
    return jnp.take_along_axis(listing, (jnp.arange(top)[None, :] + rotation) % top, axis=1)


def shares(count, total, limit, skew, full):
    portions = [(1 << 20) // math.isqrt(rank ** skew) + 1 for rank in range(1, count + 1)]
    largest = limit if full else min(limit, max(-(-total // count), total * portions[0] // sum(portions)))
    least = 1 if total - largest >= count - 1 else 0
    holding, spare = [largest] + [least] * (count - 1), total - largest - least * (count - 1)
    while spare > 0:
        free = [i for i in range(1, count) if holding[i] < largest] or [i for i in range(1, count) if holding[i] < limit]
        pool, left = sum([portions[i] for i in free]), spare
        for i in free:
            addition = min(limit - holding[i], max(1, left * portions[i] // pool), spare)
            holding[i] = holding[i] + addition
            spare = spare - addition
    return np.array(holding)


def gaussian(stream_key, shape, scale, bound, shards=(), kind=jnp.bfloat16):
    gain = steps_of(stream_key, shape, shards, -0.22, 0.18) if shards else 1.0
    array = jax.random.normal(stream_key, shape, jnp.float32) * scale * gain
    return jnp.minimum(jnp.maximum(array, -bound), bound).astype(kind)


def setup_inputs(seed: int = 0, part: int = 0) -> dict:
    arg_keys = jax.random.split(jax.random.key(seed), 20)
    part_splits = jax.random.split(jax.random.fold_in(arg_keys[19], part), 20)
    holder_keys = jax.random.split(jax.random.fold_in(part_splits[0], 1), QUERY_COUNT_ALL // REQ_DEV)
    holder_turns = jax.random.permutation(jax.random.fold_in(part_splits[0], 3), QUERY_COUNT_ALL // REQ_DEV)
    holder = jax.vmap(lambda own, number: routed_block(jax.random.fold_in(part_splits[0], 2), own, number, REQ_DEV, N_REPLICA, 1, PAIR, 2))(holder_keys, holder_turns).reshape((QUERY_COUNT_ALL, 1))
    cache_slot = with_ends(jax.random.randint(part_splits[1], (QUERY_COUNT_ALL,), 0, SLOTS), jax.random.fold_in(part_splits[1], 1), 0, SLOTS - 1).astype(jnp.int32)
    prefix_pages = draw_prefix_pages(jax.random.fold_in(jax.random.fold_in(arg_keys[19], part), 71), part)
    page_ids = with_ends(jax.random.randint(part_splits[3], (QUERY_COUNT_ALL, MAXP), 0, POOL), jax.random.fold_in(part_splits[3], 1), 0, POOL - 1).astype(jnp.int32)
    suffix_length = draw_suffix_length(jax.random.fold_in(jax.random.fold_in(arg_keys[19], part), 71), part)
    cache_states = gaussian(part_splits[5], (CACHED, SSM_HEADS, SSM_HDIM, STATE), 0.1, 0.59765625, ((0, 4), (1, 4)))
    page_keys = gaussian(part_splits[6], (PAGES_ALL, PAGE, KV_HEADS * HEAD_DIM), 1.0, 5.0, ((0, 4), (2, 4)))
    page_values = gaussian(part_splits[7], (PAGES_ALL, PAGE, KV_HEADS * HEAD_DIM), 1.0, 5.0, ((0, 4), (2, 4)))
    ssm_inputs = gaussian(part_splits[8], (QUERY_COUNT_ALL, TAIL_SPOTS, SSM_HEADS * SSM_HDIM), 1.0, 6.0, ((0, 4), (2, 4)))
    step_sizes = draw_step_sizes(jax.random.fold_in(jax.random.fold_in(arg_keys[19], part), 71), part)
    log_rates = jnp.clip(jax.random.uniform(arg_keys[10], (SSM_HEADS,), jnp.float32, -0.5, 0.5) * steps_of(arg_keys[10], (SSM_HEADS,), ((0, 4),), -0.4, 0.0), -0.5, 0.5)
    write_map = gaussian(part_splits[11], (QUERY_COUNT_ALL, TAIL_SPOTS, GROUPS * STATE), 1.0, 6.0, ((0, 4), (2, 4)))
    read_map = gaussian(part_splits[12], (QUERY_COUNT_ALL, TAIL_SPOTS, GROUPS * STATE), 1.0, 6.0, ((0, 4), (2, 4)))
    skip_gain = jnp.clip(0.5 + 1.0 * jax.random.uniform(arg_keys[13], (SSM_HEADS,), jnp.float32) ** steps_of(arg_keys[13], (SSM_HEADS,), ((0, 4),), -0.2, 0.2), 0.5, 1.5)
    gate_values = draw_gate_values(jax.random.fold_in(jax.random.fold_in(arg_keys[19], part), 71), part)
    norm_gain = jnp.clip(1.0 + 0.15 * jax.random.normal(arg_keys[15], (SSM_HEADS * SSM_HDIM,), jnp.float32), 0.25, 1.75)
    queries = draw_queries(jax.random.fold_in(jax.random.fold_in(arg_keys[19], part), 71), part)
    suffix_keys = draw_suffix_keys(jax.random.fold_in(jax.random.fold_in(arg_keys[19], part), 71), part)
    suffix_values = gaussian(part_splits[18], (QUERY_COUNT_ALL, TAIL_SPOTS, KV_HEADS * HEAD_DIM), 1.0, 5.0, ((0, 4), (2, 4)))
    return dict(holder=holder, cache_slot=cache_slot, prefix_pages=prefix_pages, page_ids=page_ids, suffix_length=suffix_length, cache_states=cache_states, page_keys=page_keys, page_values=page_values, ssm_inputs=ssm_inputs, step_sizes=step_sizes, log_rates=log_rates, write_map=write_map, read_map=read_map, skip_gain=skip_gain, gate_values=gate_values, norm_gain=norm_gain, queries=queries, suffix_keys=suffix_keys, suffix_values=suffix_values)


def mamba_request(request_items, cache_states, log_rates, skip_gain, norm_gain):
    inputs, step_rows, write_rows, read_rows, gate_rows, state_index, live_count = request_items
    head_count = log_rates.shape[0]
    head_width = inputs.shape[1] // head_count
    positions = inputs.shape[0]
    per_group = head_count // GROUPS
    start_state = cache_states[state_index]
    decays = step_rows * (-jnp.exp(log_rates))[None, :]
    running = jnp.cumsum(decays, axis=0)
    position = jnp.arange(positions)
    causal = position[:, None] >= position[None, :]
    spread = jnp.where(causal[:, :, None], running[:, None, :] - running[None, :, :], -1e+30)
    write_group = write_rows.astype(jnp.float32).reshape(positions, GROUPS, -1)
    read_group = read_rows.astype(jnp.float32).reshape(positions, GROUPS, -1)
    contact = jnp.einsum('tgn,sgn->tsg', read_group, write_group)
    contact = jnp.repeat(contact, per_group, axis=2)
    mixing = (jnp.exp(spread) * contact * step_rows[None, :, :]).astype(jnp.bfloat16)
    input_heads = inputs.astype(jnp.float32).reshape(positions, head_count, head_width)
    within = jnp.einsum('tsh,shp->thp', mixing.astype(jnp.float32), input_heads)
    read_heads = jnp.repeat(read_group, per_group, axis=1)
    carried = jnp.einsum('thn,hpn->thp', read_heads, start_state.astype(jnp.float32)).astype(jnp.bfloat16)
    combined = within + jnp.exp(running)[:, :, None] * carried.astype(jnp.float32) + skip_gain[None, :, None] * input_heads
    gated = combined.reshape(positions, GROUPS, -1) * jax.nn.silu(gate_rows.astype(jnp.float32)).reshape(positions, GROUPS, -1)
    inverse_rms = lax.rsqrt(lax.optimization_barrier(jnp.mean(gated * gated, axis=-1, keepdims=True)) + 1e-05)
    normalized = (gated * inverse_rms).reshape(positions, -1) * norm_gain[None, :]
    valid_rows = position < live_count
    return jnp.where(valid_rows[:, None], normalized, 0.0).astype(jnp.bfloat16)

def attend_request(request_items, page_keys, page_values):
    query_rows, key_rows, value_rows, page_rows, page_count, live_count = request_items
    positions = query_rows.shape[0]
    per_kv = Q_HEADS // KV_HEADS
    cached_keys = page_keys[page_rows].reshape(MAXP * PAGE, -1)
    cached_values = page_values[page_rows].reshape(MAXP * PAGE, -1)
    all_keys = jnp.concatenate([cached_keys, key_rows], axis=0).astype(jnp.float32).reshape(-1, KV_HEADS, HEAD_DIM)
    all_values = jnp.concatenate([cached_values, value_rows], axis=0).astype(jnp.float32).reshape(-1, KV_HEADS, HEAD_DIM)
    query_heads = query_rows.astype(jnp.float32).reshape(positions, KV_HEADS, per_kv, HEAD_DIM)
    scores = jnp.einsum('tgqd,kgd->tgqk', query_heads, all_keys) / math.sqrt(HEAD_DIM)
    position = jnp.arange(positions)
    key_index = jnp.arange(all_keys.shape[0])
    cached = MAXP * PAGE
    allowed = jnp.where(key_index[None, :] < cached, key_index[None, :] < page_count * PAGE, key_index[None, :] - cached <= position[:, None])
    scores = jnp.where(allowed[:, None, None, :], scores, -1e+30)
    row_max = lax.optimization_barrier(jnp.max(scores, axis=-1, keepdims=True))
    expo = jnp.exp(scores - row_max)
    weights = (expo / lax.optimization_barrier(jnp.sum(expo, axis=-1, keepdims=True))).astype(jnp.bfloat16)
    attended = jnp.einsum('tgqk,kgd->tgqd', weights.astype(jnp.float32), all_values).reshape(positions, -1)
    valid_rows = position < live_count
    return jnp.where(valid_rows[:, None], attended, 0.0).astype(jnp.bfloat16)

def reference(holder, cache_slot, prefix_pages, page_ids, suffix_length, cache_states, page_keys, page_values, ssm_inputs, step_sizes, log_rates, write_map, read_map, skip_gain, gate_values, norm_gain, queries, suffix_keys, suffix_values):
    holders = holder[:, 0].astype(jnp.int32)
    state_index = (holders * SLOTS + cache_slot).astype(jnp.int32)
    page_rows = (holders[:, None] * POOL + page_ids).astype(jnp.int32)
    mamba_output = lax.map(lambda request_items: mamba_request(request_items, cache_states, log_rates, skip_gain, norm_gain), (ssm_inputs, step_sizes, write_map, read_map, gate_values, state_index, suffix_length))
    attention_output = lax.map(lambda request_items: attend_request(request_items, page_keys, page_values), (queries, suffix_keys, suffix_values, page_rows, prefix_pages, suffix_length))
    return (mamba_output, attention_output)
```

```python
import functools
import math

import jax
import jax.numpy as jnp
from jax import lax
from jax.experimental import pallas as pl
from jax.experimental.pallas import tpu as pltpu
from jax.sharding import PartitionSpec as P

STATE = 128
HEAD_DIM = 128
MIB = 1 << 20

ANY = pl.BlockSpec(memory_space=pl.ANY)
SMEM = pl.BlockSpec(memory_space=pltpu.SMEM)


def partner_steps(replicas):
    return list(range(replicas - 1, 0, -1))


def route_kernel(
    replicas,
    slots,
    count,
    most,
    page_len,
    me_ref,
    holder_ref,
    slot_ref,
    pages_ref,
    keys_ref,
    values_ref,
    reads_ref,
    *outs,
):
    steps = partner_steps(replicas)
    page_out = dict(zip(steps, outs[: replicas - 1]))
    read_out = dict(zip(steps + [0], outs[replicas - 1 : 2 * replicas - 1]))
    state_slot, source, rank, order, ends = outs[2 * replicas - 1 : 2 * replicas + 4]
    page_sem, read_sem, seen = outs[2 * replicas + 4 :]
    me = me_ref[0]

    def page_copy(array, page, out, slot, kind, place):
        return pltpu.make_async_copy(
            array.at[page],
            out.at[slot, kind, pl.ds(pl.multiple_of(place * page_len, page_len), page_len)],
            page_sem,
        )

    def clear(i, carry):
        state_slot[i] = 0
        return carry

    lax.fori_loop(0, replicas * slots, clear, 0)
    sent = jnp.int32(0)
    for step in steps + [0]:
        first = lax.bitwise_xor(me, step) * count

        def serve(j, rank_here, step=step, first=first):
            request = first + j
            hit = holder_ref[request] == me
            slot = jnp.minimum(rank_here, slots - 1)

            @pl.when(hit)
            def _():
                state_slot[step * slots + slot] = slot_ref[request]
                if step:
                    for place in range(most):
                        page = pages_ref[request * most + place]
                        page_copy(keys_ref, page, page_out[step], slot, 0, place).start()
                        page_copy(values_ref, page, page_out[step], slot, 1, place).start()

            return rank_here + hit.astype(jnp.int32)

        found = lax.fori_loop(0, count, serve, jnp.int32(0))
        if step:
            sent = sent + found

    def clear_seen(i, carry):
        seen[i] = 0
        return carry

    lax.fori_loop(0, replicas, clear_seen, 0)

    def ask(j, carry):
        step = lax.bitwise_xor(me, holder_ref[me * count + j])
        slot = jnp.minimum(seen[step], slots - 1)
        seen[step] = slot + 1
        source[j] = step
        rank[j] = slot
        for known in steps + [0]:

            @pl.when(step == known)
            def _(known=known):
                pltpu.make_async_copy(reads_ref.at[j], read_out[known].at[slot], read_sem).start()

        return carry

    lax.fori_loop(0, count, ask, 0)
    place = jnp.int32(0)
    for step in range(replicas):

        def put(j, at, step=step):
            hit = source[j] == step

            @pl.when(hit)
            def _():
                order[at] = j

            return at + hit.astype(jnp.int32)

        place = lax.fori_loop(0, count, put, place)
        ends[step] = place

    def wait_page(i, carry):
        page_copy(keys_ref, 0, page_out[steps[0]], 0, 0, 0).wait()
        return carry

    lax.fori_loop(0, sent * (2 * most), wait_page, 0)

    def wait_read(i, carry):
        pltpu.make_async_copy(reads_ref.at[0], read_out[0].at[0], read_sem).wait()
        return carry

    lax.fori_loop(0, count, wait_read, 0)


def carried_kernel(slot_ref, read_ref, state_ref, out_ref):
    out_ref[0] = lax.dot_general(
        read_ref[0],
        state_ref[0],
        (((1,), (1,)), ((), ())),
        preferred_element_type=jnp.float32,
    ).astype(out_ref.dtype)


def attention_kernel(
    replicas,
    kv_here,
    per_kv,
    page_len,
    most,
    source_ref,
    rank_ref,
    count_ref,
    live_ref,
    pages_ref,
    query_ref,
    key_ref,
    value_ref,
    *rest,
):
    steps = partner_steps(replicas)
    arrived = dict(zip(steps, rest[: replicas - 1]))
    pool_keys, pool_values, out_ref, buffer, sems = rest[replicas - 1 :]
    i, total = pl.program_id(0), pl.num_programs(0)

    def fetch(j, slot):
        step, rank = source_ref[j], rank_ref[j]
        for known in steps:

            @pl.when(step == known)
            def _(known=known):
                pltpu.make_async_copy(arrived[known].at[rank], buffer.at[slot], sems.at[slot]).start()

        @pl.when(step == 0)
        def _():
            for place in range(most):
                page = pages_ref[j * most + place]
                rows = pl.ds(place * page_len, page_len)
                pltpu.make_async_copy(pool_keys.at[page], buffer.at[slot, 0, rows], sems.at[slot]).start()
                pltpu.make_async_copy(pool_values.at[page], buffer.at[slot, 1, rows], sems.at[slot]).start()

    @pl.when(i == 0)
    def _():
        fetch(i, 0)

    @pl.when(i + 1 < total)
    def _():
        fetch(i + 1, lax.rem(i + 1, 2))

    now = lax.rem(i, 2)
    pltpu.make_async_copy(buffer.at[now], buffer.at[now], sems.at[now]).wait()

    positions = query_ref.shape[1]
    rows = per_kv * positions
    cached = most * page_len
    live = live_ref[i]
    scale = 1.0 / math.sqrt(HEAD_DIM)
    column = lax.broadcasted_iota(jnp.int32, (rows, cached), 1)
    ahead = column < count_ref[i] * page_len
    row = lax.broadcasted_iota(jnp.int32, (rows, positions), 0) & (positions - 1)
    causal = lax.broadcasted_iota(jnp.int32, (rows, positions), 1) <= row
    alive = (lax.broadcasted_iota(jnp.int32, (rows, HEAD_DIM), 0) & (positions - 1)) < live
    contract = (((1,), (1,)), ((), ()))
    for g in range(kv_here):
        lanes = slice(g * HEAD_DIM, (g + 1) * HEAD_DIM)
        heads = [(g * per_kv + q) * HEAD_DIM for q in range(per_kv)]
        query = jnp.concatenate([query_ref[0, :, h : h + HEAD_DIM] for h in heads], axis=0)
        old_keys, old_values = buffer[now, 0, :, lanes], buffer[now, 1, :, lanes]
        new_keys, new_values = key_ref[0, :, lanes], value_ref[0, :, lanes]
        old = lax.dot_general(query, old_keys, contract, preferred_element_type=jnp.float32) * scale
        new = lax.dot_general(query, new_keys, contract, preferred_element_type=jnp.float32) * scale
        old = jnp.where(ahead, old, -1e30)
        new = jnp.where(causal, new, -1e30)
        top = jnp.maximum(jnp.max(old, axis=1, keepdims=True), jnp.max(new, axis=1, keepdims=True))
        old, new = jnp.exp(old - top), jnp.exp(new - top)
        share = 1.0 / (jnp.sum(old, axis=1, keepdims=True) + jnp.sum(new, axis=1, keepdims=True))
        old, new = (old * share).astype(jnp.bfloat16), (new * share).astype(jnp.bfloat16)
        result = jnp.dot(old, old_values, preferred_element_type=jnp.float32) + jnp.dot(
            new, new_values, preferred_element_type=jnp.float32
        )
        result = jnp.where(alive, result, 0.0).astype(out_ref.dtype)
        for q, h in enumerate(heads):
            out_ref[0, :, h : h + HEAD_DIM] = result[q * positions : (q + 1) * positions]


def halves(x):
    high = x.astype(jnp.bfloat16)
    return high, (x - high.astype(jnp.float32)).astype(jnp.bfloat16)


def within_kernel(
    rate_ref, skip_ref, spread_ref, step_ref, read_ref, write_ref, input_ref, gate_ref, fixed_ref, scaled_ref
):
    positions = input_ref.shape[1]
    heads = step_ref.shape[2]
    step = step_ref[0]
    later = lax.broadcasted_iota(jnp.int32, (positions, positions), 0)
    earlier = lax.broadcasted_iota(jnp.int32, (positions, positions), 1)
    causal = earlier <= later
    decays = step * (-jnp.exp(rate_ref[...]))
    running = lax.dot_general(
        causal.astype(jnp.float32),
        decays,
        (((1,), (0,)), ((), ())),
        precision=lax.Precision.HIGHEST,
        preferred_element_type=jnp.float32,
    )
    decay = jnp.exp(running)
    growth = jnp.exp(-running) * step
    both = jnp.concatenate([decay, growth], axis=0)
    high, low = halves(both)
    wide = jnp.dot(
        jnp.concatenate([high, low], axis=1), spread_ref[...], preferred_element_type=jnp.float32
    )
    decay, growth = wide[:positions], wide[positions:]
    contact = lax.dot_general(
        read_ref[0], write_ref[0], (((1,), (1,)), ((), ())), preferred_element_type=jnp.float32
    )
    contact = jnp.where(causal, contact, 0.0)
    contact_high, contact_low = halves(contact)
    inputs = input_ref[0].astype(jnp.float32)
    weighed = (inputs * growth).astype(jnp.bfloat16)
    within = jnp.dot(
        jnp.concatenate([contact_high, contact_low], axis=1),
        jnp.concatenate([weighed, weighed], axis=0),
        preferred_element_type=jnp.float32,
    )
    gate = gate_ref[0].astype(jnp.float32)
    gate = gate / (1.0 + jnp.exp(-gate))
    fixed_ref[0] = gate * (decay * within + skip_ref[...] * inputs)
    scaled_ref[0] = gate * decay


def finish_kernel(
    members, phase, order_ref, source_ref, rank_ref, live_ref, span_ref, gain_ref, fixed_ref, scaled_ref, *rest
):
    arrived = dict(zip(members, rest[: len(members)]))
    out_ref, buffer, sems = rest[len(members) + phase :]
    i = pl.program_id(0)
    first, total = span_ref[0], span_ref[1] - span_ref[0]

    def fetch(at, slot):
        request = order_ref[first + at]
        for known in members:

            @pl.when(source_ref[request] == known)
            def _(known=known):
                pltpu.make_async_copy(
                    arrived[known].at[rank_ref[request]], buffer.at[slot], sems.at[slot]
                ).start()

    @pl.when((i == 0) & (total > 0))
    def _():
        fetch(i, 0)

    @pl.when(i + 1 < total)
    def _():
        fetch(i + 1, lax.rem(i + 1, 2))

    @pl.when(i < total)
    def _():
        now = lax.rem(i, 2)
        pltpu.make_async_copy(buffer.at[now], buffer.at[now], sems.at[now]).wait()
        positions, channels = fixed_ref.shape[1:]
        live = live_ref[order_ref[first + i]]
        gated = fixed_ref[0] + scaled_ref[0] * buffer[now].astype(jnp.float32)
        square = jnp.sum(gated * gated, axis=1, keepdims=True) * (1.0 / channels)
        alive = lax.broadcasted_iota(jnp.int32, (positions, 1), 0) < live
        factor = lax.rsqrt(square + 1e-05)
        out_ref[0] = jnp.where(alive, gated * factor * gain_ref[...], 0.0).astype(out_ref.dtype)

    if phase:

        @pl.when((i == 0) & (total == 0))
        def _():
            last = order_ref[order_ref.shape[0] - 1]
            keep = pltpu.make_async_copy(rest[len(members)].at[last], out_ref.at[0], sems.at[0])
            keep.start()
            keep.wait()


def per_device(
    holder,
    cache_slot,
    prefix_pages,
    page_ids,
    suffix_length,
    cache_states,
    page_keys,
    page_values,
    ssm_inputs,
    step_sizes,
    log_rates,
    write_map,
    read_map,
    skip_gain,
    gate_values,
    norm_gain,
    queries,
    suffix_keys,
    suffix_values,
):
    replicas = lax.axis_size("replica")
    assert replicas & (replicas - 1) == 0
    myself = lax.axis_index("replica").astype(jnp.int32)
    count, positions, channels = ssm_inputs.shape
    slots = (count + replicas - 1) // replicas
    heads = log_rates.shape[0]
    width = channels // heads
    assert write_map.shape[2] == STATE
    page_len, row_width = page_keys.shape[1:]
    most = page_ids.shape[1]
    kv_here = row_width // HEAD_DIM
    per_kv = queries.shape[2] // row_width
    bf16, f32 = jnp.bfloat16, jnp.float32
    steps = partner_steps(replicas)
    shape = jax.ShapeDtypeStruct

    routed = pl.pallas_call(
        functools.partial(route_kernel, replicas, slots, count, most, page_len),
        out_shape=[shape((slots, 2, most * page_len, row_width), bf16)] * (replicas - 1)
        + [shape((slots, positions, STATE), bf16)] * replicas
        + [
            shape((replicas * slots,), jnp.int32),
            shape((count,), jnp.int32),
            shape((count,), jnp.int32),
            shape((count,), jnp.int32),
            shape((replicas,), jnp.int32),
        ],
        in_specs=[SMEM] * 4 + [ANY] * 3,
        out_specs=[ANY] * (2 * replicas - 1) + [SMEM] * 5,
        scratch_shapes=[pltpu.SemaphoreType.DMA, pltpu.SemaphoreType.DMA, pltpu.SMEM((replicas,), jnp.int32)],
        name="route",
    )(
        myself.reshape(1),
        holder.reshape(-1),
        cache_slot,
        page_ids.reshape(-1),
        page_keys,
        page_values,
        read_map,
    )
    send_pages = dict(zip(steps, routed[: replicas - 1]))
    send_reads = dict(zip(steps + [0], routed[replicas - 1 : 2 * replicas - 1]))
    state_slot, source, rank, order, ends = routed[2 * replicas - 1 :]

    def exchange(x, step):
        return lax.ppermute(x, "replica", [(i, i ^ step) for i in range(replicas)])

    reads = {s: exchange(send_reads[s], s) for s in steps}
    reads[0] = send_reads[0]
    pages = {s: exchange(send_pages[s], s) for s in steps}

    states = cache_states.reshape(cache_states.shape[0], channels, STATE)
    carried = {}
    for s in steps + [0]:
        carried[s] = pl.pallas_call(
            carried_kernel,
            out_shape=shape((slots, positions, channels), bf16),
            grid_spec=pltpu.PrefetchScalarGridSpec(
                num_scalar_prefetch=1,
                grid=(slots,),
                in_specs=[
                    pl.BlockSpec((1, positions, STATE), lambda i, slot: (i, 0, 0)),
                    pl.BlockSpec((1, channels, STATE), lambda i, slot: (slot[i], 0, 0)),
                ],
                out_specs=pl.BlockSpec((1, positions, channels), lambda i, slot: (i, 0, 0)),
            ),
            cost_estimate=pl.CostEstimate(
                flops=2 * slots * positions * channels * STATE,
                bytes_accessed=2 * slots * channels * (STATE + positions),
                transcendentals=0,
            ),
            name="carried",
        )(lax.slice(state_slot, (s * slots,), ((s + 1) * slots,)), reads[s], states)
        if s:
            carried[s] = exchange(carried[s], s)

    spread = (jnp.arange(2 * heads)[:, None] % heads == jnp.arange(channels)[None, :] // width).astype(bf16)
    row = lambda i: (i, 0, 0)
    whole = lambda i: (0, 0)
    fixed, scaled = pl.pallas_call(
        within_kernel,
        out_shape=[shape((count, positions, channels), f32)] * 2,
        grid=(count,),
        in_specs=[
            pl.BlockSpec((1, heads), whole),
            pl.BlockSpec((1, channels), whole),
            pl.BlockSpec((2 * heads, channels), whole),
            pl.BlockSpec((1, positions, heads), row),
            pl.BlockSpec((1, positions, STATE), row),
            pl.BlockSpec((1, positions, STATE), row),
            pl.BlockSpec((1, positions, channels), row),
            pl.BlockSpec((1, positions, channels), row),
        ],
        out_specs=[pl.BlockSpec((1, positions, channels), row)] * 2,
        cost_estimate=pl.CostEstimate(
            flops=2 * count * positions * channels * positions * 8,
            bytes_accessed=count * positions * channels * 12,
            transcendentals=count * positions * channels,
        ),
        name="within",
    )(
        log_rates.reshape(1, heads),
        jnp.repeat(skip_gain, width).reshape(1, channels),
        spread,
        step_sizes,
        read_map,
        write_map,
        ssm_inputs,
        gate_values,
    )

    row5 = lambda i, *refs: (i, 0, 0)
    attention_output = pl.pallas_call(
        functools.partial(attention_kernel, replicas, kv_here, per_kv, page_len, most),
        out_shape=shape((count, positions, queries.shape[2]), bf16),
        grid_spec=pltpu.PrefetchScalarGridSpec(
            num_scalar_prefetch=5,
            grid=(count,),
            in_specs=[
                pl.BlockSpec((1, positions, queries.shape[2]), row5),
                pl.BlockSpec((1, positions, row_width), row5),
                pl.BlockSpec((1, positions, row_width), row5),
            ]
            + [ANY] * (replicas + 1),
            out_specs=pl.BlockSpec((1, positions, queries.shape[2]), row5),
            scratch_shapes=[
                pltpu.VMEM((2, 2, most * page_len, row_width), bf16),
                pltpu.SemaphoreType.DMA((2,)),
            ],
        ),
        cost_estimate=pl.CostEstimate(
            flops=4 * count * positions * queries.shape[2] * (most * page_len + positions),
            bytes_accessed=count * (positions * queries.shape[2] * 4 + most * page_len * row_width * 4),
            transcendentals=count * positions * kv_here * per_kv * (most * page_len + positions),
        ),
        name="attention",
    )(
        source,
        rank,
        prefix_pages,
        suffix_length,
        lax.dynamic_slice_in_dim(page_ids, myself * count, count, 0).reshape(-1),
        queries,
        suffix_keys,
        suffix_values,
        *[pages[s] for s in steps],
        page_keys,
        page_values,
    )

    mamba_output = None
    early = steps[replicas // 2 :] + [0]
    late = steps[: replicas // 2]
    middle = ends[replicas // 2 - 1]
    for phase, members in enumerate([early, late]):
        span = jnp.stack([middle, ends[replicas - 1]] if phase else [jnp.zeros_like(middle), middle])

        def place(i, order, source, rank, live, span):
            at = jnp.minimum(span[0] + i, jnp.maximum(span[1] - 1, 0))
            return (order[at], 0, 0)

        mamba_output = pl.pallas_call(
            functools.partial(finish_kernel, members, phase),
            out_shape=shape((count, positions, channels), bf16),
            grid_spec=pltpu.PrefetchScalarGridSpec(
                num_scalar_prefetch=5,
                grid=(min(count, slots * len(members)),),
                in_specs=[
                    pl.BlockSpec((1, channels), lambda i, *refs: (0, 0)),
                    pl.BlockSpec((1, positions, channels), place),
                    pl.BlockSpec((1, positions, channels), place),
                ]
                + [ANY] * (len(members) + phase),
                out_specs=pl.BlockSpec((1, positions, channels), place),
                scratch_shapes=[
                    pltpu.VMEM((2, positions, channels), bf16),
                    pltpu.SemaphoreType.DMA((2,)),
                ],
            ),
            input_output_aliases={8 + len(members): 0} if phase else {},
            cost_estimate=pl.CostEstimate(
                flops=6 * count * positions * channels,
                bytes_accessed=count * positions * channels * 6,
                transcendentals=0,
            ),
            name="finish",
        )(
            order,
            source,
            rank,
            suffix_length,
            span,
            norm_gain.reshape(1, channels),
            fixed,
            scaled,
            *[carried[s] for s in members],
            *([mamba_output] if phase else []),
        )
    return (mamba_output, attention_output)


def solution(mesh):
    return jax.shard_map(
        per_device,
        mesh=mesh,
        in_specs=(
            P("groups", None),
            P("groups"),
            P(("groups", "replica")),
            P("groups", None),
            P(("groups", "replica")),
            P(("groups", "replica"), "tensor", None, None),
            P(("groups", "replica"), None, "tensor"),
            P(("groups", "replica"), None, "tensor"),
            P(("groups", "replica"), None, "tensor"),
            P(("groups", "replica"), None, "tensor"),
            P("tensor"),
            P(("groups", "replica"), None, "tensor"),
            P(("groups", "replica"), None, "tensor"),
            P("tensor"),
            P(("groups", "replica"), None, "tensor"),
            P("tensor"),
            P(("groups", "replica"), None, "tensor"),
            P(("groups", "replica"), None, "tensor"),
            P(("groups", "replica"), None, "tensor"),
        ),
        out_specs=(
            P(("groups", "replica"), None, "tensor"),
            P(("groups", "replica"), None, "tensor"),
        ),
        check_vma=False,
    )
```

```python
import functools
import math

import jax
import jax.numpy as jnp
from jax import lax
from jax.experimental import pallas as pl
from jax.experimental.pallas import tpu as pltpu
from jax.sharding import PartitionSpec as P

STATE = 128
HEAD_DIM = 128
MIB = 1 << 20

ANY = pl.BlockSpec(memory_space=pl.ANY)
VMEM = pl.BlockSpec(memory_space=pltpu.VMEM)
SMEM = pl.BlockSpec(memory_space=pltpu.SMEM)
PARAMS = pltpu.CompilerParams(vmem_limit_bytes=56 * MIB)


def partner_steps(replicas):
    return list(range(replicas - 1, 0, -1))


def route_kernel(
    replicas, slots, count, most, page_len, me_ref, holder_ref, pages_ref, keys_hbm, values_hbm, *rest
):
    steps = partner_steps(replicas)
    page_out = dict(zip(steps, rest[: replicas - 1]))
    token, keys, values, packed, sems = rest[replicas - 1 :]
    loads = [
        pltpu.make_async_copy(keys_hbm, keys, sems.at[0]),
        pltpu.make_async_copy(values_hbm, values, sems.at[1]),
    ]
    for load in loads:
        load.start()
    me = me_ref[0]
    token[0] = me
    for load in loads:
        load.wait()
    copies = []
    for at, step in enumerate(steps):
        first = lax.bitwise_xor(me, step) * count

        def serve(j, rank_here, at=at, first=first):
            request = first + j
            hit = holder_ref[0, request] == me

            @pl.when(hit)
            def _():
                slot = jnp.minimum(rank_here, slots - 1)
                for place in range(most):
                    page = pages_ref[place, request]
                    rows = slice(place * page_len, (place + 1) * page_len)
                    packed[at, slot, 0, rows, :] = keys[page]
                    packed[at, slot, 1, rows, :] = values[page]

            return rank_here + hit.astype(jnp.int32)

        lax.fori_loop(0, count, serve, jnp.int32(0))
        copies.append(pltpu.make_async_copy(packed.at[at], page_out[step], sems.at[2 + at]))
        copies[-1].start()
    for copy in copies:
        copy.wait()


def places(replicas, slots, count):
    state = 0
    source = state + replicas * slots
    rank = source + count
    order = rank + count
    ends = order + count
    return state, source, rank, order, ends, ends + replicas


def plan_kernel(replicas, slots, count, me_ref, token_ref, holder_ref, slot_ref, reads_hbm, *rest):
    steps = partner_steps(replicas)
    read_out = dict(zip(steps, rest[: replicas - 1]))
    plan, seen, reads, sems = rest[replicas - 1 :]
    state, source, rank, order, ends, mine = places(replicas, slots, count)
    load = pltpu.make_async_copy(reads_hbm, reads, sems.at[0])
    load.start()
    me = me_ref[0]
    plan[mine] = me

    def clear(i, carry):
        plan[state + i] = 0
        return carry

    lax.fori_loop(0, replicas * slots, clear, 0)

    def clear_seen(i, carry):
        seen[i] = 0
        return carry

    lax.fori_loop(0, replicas, clear_seen, 0)
    load.wait()

    def ask(j, carry):
        step = lax.bitwise_xor(me, holder_ref[0, me * count + j])
        slot = jnp.minimum(seen[step], slots - 1)
        seen[step] = slot + 1
        plan[source + j] = step
        plan[rank + j] = slot
        for known in steps:

            @pl.when(step == known)
            def _(known=known):
                pltpu.make_async_copy(reads.at[j], read_out[known].at[slot], sems.at[1]).start()

        return carry

    lax.fori_loop(0, count, ask, 0)
    for step in steps + [0]:
        first = lax.bitwise_xor(me, step) * count

        def serve(j, rank_here, step=step, first=first):
            hit = holder_ref[0, first + j] == me

            @pl.when(hit)
            def _():
                plan[state + step * slots + jnp.minimum(rank_here, slots - 1)] = slot_ref[first + j]

            return rank_here + hit.astype(jnp.int32)

        lax.fori_loop(0, count, serve, jnp.int32(0))
    place = jnp.int32(0)
    for step in range(replicas):

        def put(j, at, step=step):
            hit = plan[source + j] == step

            @pl.when(hit)
            def _():
                plan[order + at] = j

            return at + hit.astype(jnp.int32)

        place = lax.fori_loop(0, count, put, place)
        plan[ends + step] = place

    def wait_read(i, carry):
        pltpu.make_async_copy(reads.at[0], read_out[steps[0]].at[0], sems.at[1]).wait()
        return carry

    lax.fori_loop(0, count - plan[ends], wait_read, 0)


def carried_kernel(slot_ref, read_ref, state_ref, out_ref):
    out_ref[0] = lax.dot_general(
        read_ref[0],
        state_ref[0],
        (((1,), (1,)), ((), ())),
        preferred_element_type=jnp.float32,
    ).astype(out_ref.dtype)


def attention_kernel(
    replicas,
    kv_here,
    per_kv,
    page_len,
    most,
    slots,
    plan_ref,
    count_ref,
    live_ref,
    pages_ref,
    query_ref,
    key_ref,
    value_ref,
    *rest,
):
    steps = partner_steps(replicas)
    arrived = dict(zip(steps, rest[: replicas - 1]))
    pool_keys, pool_values, out_ref, buffer, sems = rest[replicas - 1 :]
    i, total = pl.program_id(0), pl.num_programs(0)
    _, at_source, at_rank, _, _, at_me = places(replicas, slots, count_ref.shape[0])

    def fetch(j, slot):
        step, rank = plan_ref[at_source + j], plan_ref[at_rank + j]
        request = plan_ref[at_me] * count_ref.shape[0] + j
        for known in steps:

            @pl.when(step == known)
            def _(known=known):
                pltpu.make_async_copy(arrived[known].at[rank], buffer.at[slot], sems.at[slot]).start()

        @pl.when(step == 0)
        def _():
            for place in range(most):
                page = pages_ref[place, request]
                rows = pl.ds(place * page_len, page_len)
                pltpu.make_async_copy(pool_keys.at[page], buffer.at[slot, 0, rows], sems.at[slot]).start()
                pltpu.make_async_copy(pool_values.at[page], buffer.at[slot, 1, rows], sems.at[slot]).start()

    @pl.when(i == 0)
    def _():
        fetch(i, 0)

    @pl.when(i + 1 < total)
    def _():
        fetch(i + 1, lax.rem(i + 1, 2))

    now = lax.rem(i, 2)
    pltpu.make_async_copy(buffer.at[now], buffer.at[now], sems.at[now]).wait()

    positions = query_ref.shape[1]
    rows = per_kv * positions
    cached = most * page_len
    live = live_ref[i]
    scale = 1.0 / math.sqrt(HEAD_DIM)
    column = lax.broadcasted_iota(jnp.int32, (rows, cached), 1)
    ahead = column < count_ref[i] * page_len
    row = lax.broadcasted_iota(jnp.int32, (rows, positions), 0) & (positions - 1)
    causal = lax.broadcasted_iota(jnp.int32, (rows, positions), 1) <= row
    alive = (lax.broadcasted_iota(jnp.int32, (rows, HEAD_DIM), 0) & (positions - 1)) < live
    contract = (((1,), (1,)), ((), ()))
    for g in range(kv_here):
        lanes = slice(g * HEAD_DIM, (g + 1) * HEAD_DIM)
        heads = [(g * per_kv + q) * HEAD_DIM for q in range(per_kv)]
        query = jnp.concatenate([query_ref[0, :, h : h + HEAD_DIM] for h in heads], axis=0)
        old_keys, old_values = buffer[now, 0, :, lanes], buffer[now, 1, :, lanes]
        new_keys, new_values = key_ref[0, :, lanes], value_ref[0, :, lanes]
        old = lax.dot_general(query, old_keys, contract, preferred_element_type=jnp.float32) * scale
        new = lax.dot_general(query, new_keys, contract, preferred_element_type=jnp.float32) * scale
        old = jnp.where(ahead, old, -1e30)
        new = jnp.where(causal, new, -1e30)
        top = jnp.maximum(jnp.max(old, axis=1, keepdims=True), jnp.max(new, axis=1, keepdims=True))
        old, new = jnp.exp(old - top), jnp.exp(new - top)
        share = 1.0 / (jnp.sum(old, axis=1, keepdims=True) + jnp.sum(new, axis=1, keepdims=True))
        old, new = (old * share).astype(jnp.bfloat16), (new * share).astype(jnp.bfloat16)
        result = jnp.dot(old, old_values, preferred_element_type=jnp.float32) + jnp.dot(
            new, new_values, preferred_element_type=jnp.float32
        )
        result = jnp.where(alive, result, 0.0).astype(out_ref.dtype)
        for q, h in enumerate(heads):
            out_ref[0, :, h : h + HEAD_DIM] = result[q * positions : (q + 1) * positions]


def halves(x):
    high = x.astype(jnp.bfloat16)
    return high, (x - high.astype(jnp.float32)).astype(jnp.bfloat16)


def within_kernel(
    rate_ref, skip_ref, spread_ref, step_ref, read_ref, write_ref, input_ref, gate_ref, fixed_ref, scaled_ref
):
    positions = input_ref.shape[1]
    heads = step_ref.shape[2]
    step = step_ref[0]
    later = lax.broadcasted_iota(jnp.int32, (positions, positions), 0)
    earlier = lax.broadcasted_iota(jnp.int32, (positions, positions), 1)
    causal = earlier <= later
    decays = step * (-jnp.exp(rate_ref[...]))
    running = lax.dot_general(
        causal.astype(jnp.float32),
        decays,
        (((1,), (0,)), ((), ())),
        precision=lax.Precision.HIGHEST,
        preferred_element_type=jnp.float32,
    )
    decay = jnp.exp(running)
    growth = jnp.exp(-running) * step
    both = jnp.concatenate([decay, growth], axis=0)
    high, low = halves(both)
    wide = jnp.dot(
        jnp.concatenate([high, low], axis=1), spread_ref[...], preferred_element_type=jnp.float32
    )
    decay, growth = wide[:positions], wide[positions:]
    contact = lax.dot_general(
        read_ref[0], write_ref[0], (((1,), (1,)), ((), ())), preferred_element_type=jnp.float32
    )
    contact = jnp.where(causal, contact, 0.0)
    contact_high, contact_low = halves(contact)
    inputs = input_ref[0].astype(jnp.float32)
    weighed = (inputs * growth).astype(jnp.bfloat16)
    within = jnp.dot(
        jnp.concatenate([contact_high, contact_low], axis=1),
        jnp.concatenate([weighed, weighed], axis=0),
        preferred_element_type=jnp.float32,
    )
    gate = gate_ref[0].astype(jnp.float32)
    gate = gate / (1.0 + jnp.exp(-gate))
    fixed_ref[0] = gate * (decay * within + skip_ref[...] * inputs)
    scaled_ref[0] = gate * decay


def span(replicas, slots, count, phase, plan):
    ends = places(replicas, slots, count)[4]
    middle = plan[ends + replicas // 2 - 1]
    return (middle, plan[ends + replicas - 1]) if phase else (jnp.zeros_like(middle), middle)


def finish_kernel(
    replicas, slots, members, phase, plan_ref, live_ref, gain_ref, fixed_ref, scaled_ref, *rest
):
    _, at_source, at_rank, at_order, _, _ = places(replicas, slots, live_ref.shape[0])
    arrived = dict(zip(members, rest[: len(members)]))
    out_ref, buffer, sems = rest[len(members) + phase :]
    i = pl.program_id(0)
    first, last = span(replicas, slots, live_ref.shape[0], phase, plan_ref)
    total = last - first

    def fetch(at, slot):
        request = plan_ref[at_order + first + at]
        for known in members:

            @pl.when(plan_ref[at_source + request] == known)
            def _(known=known):
                pltpu.make_async_copy(
                    arrived[known].at[plan_ref[at_rank + request]], buffer.at[slot], sems.at[slot]
                ).start()

    @pl.when((i == 0) & (total > 0))
    def _():
        fetch(i, 0)

    @pl.when(i + 1 < total)
    def _():
        fetch(i + 1, lax.rem(i + 1, 2))

    @pl.when(i < total)
    def _():
        now = lax.rem(i, 2)
        pltpu.make_async_copy(buffer.at[now], buffer.at[now], sems.at[now]).wait()
        positions, channels = fixed_ref.shape[1:]
        live = live_ref[plan_ref[at_order + first + i]]
        gated = fixed_ref[0] + scaled_ref[0] * buffer[now].astype(jnp.float32)
        square = jnp.sum(gated * gated, axis=1, keepdims=True) * (1.0 / channels)
        alive = lax.broadcasted_iota(jnp.int32, (positions, 1), 0) < live
        factor = lax.rsqrt(square + 1e-05)
        out_ref[0] = jnp.where(alive, gated * factor * gain_ref[...], 0.0).astype(out_ref.dtype)

    if phase:

        @pl.when((i == 0) & (total == 0))
        def _():
            last = plan_ref[at_order + live_ref.shape[0] - 1]
            keep = pltpu.make_async_copy(rest[len(members)].at[last], out_ref.at[0], sems.at[0])
            keep.start()
            keep.wait()


def per_device(
    holder,
    cache_slot,
    prefix_pages,
    page_ids,
    suffix_length,
    cache_states,
    page_keys,
    page_values,
    ssm_inputs,
    step_sizes,
    log_rates,
    write_map,
    read_map,
    skip_gain,
    gate_values,
    norm_gain,
    queries,
    suffix_keys,
    suffix_values,
):
    replicas = lax.axis_size("replica")
    assert replicas & (replicas - 1) == 0
    myself = lax.axis_index("replica").astype(jnp.int32)
    count, positions, channels = ssm_inputs.shape
    slots = (count + replicas - 1) // replicas
    heads = log_rates.shape[0]
    width = channels // heads
    assert write_map.shape[2] == STATE
    page_len, row_width = page_keys.shape[1:]
    most = page_ids.shape[1]
    kv_here = row_width // HEAD_DIM
    per_kv = queries.shape[2] // row_width
    bf16, f32 = jnp.bfloat16, jnp.float32
    steps = partner_steps(replicas)
    shape = jax.ShapeDtypeStruct

    me = myself.reshape(1)
    holder_row = holder.T
    page_rows = page_ids.T
    routed = pl.pallas_call(
        functools.partial(route_kernel, replicas, slots, count, most, page_len),
        out_shape=[shape((slots, 2, most * page_len, row_width), bf16)] * (replicas - 1)
        + [shape((1,), jnp.int32)],
        in_specs=[SMEM] * 3 + [ANY] * 2,
        out_specs=[ANY] * (replicas - 1) + [SMEM],
        scratch_shapes=[
            pltpu.VMEM(page_keys.shape, bf16),
            pltpu.VMEM(page_values.shape, bf16),
            pltpu.VMEM((replicas - 1, slots, 2, most * page_len, row_width), bf16),
            pltpu.SemaphoreType.DMA((replicas + 1,)),
        ],
        compiler_params=PARAMS,
        name="route",
    )(me, holder_row, page_rows, page_keys, page_values)
    send_pages = dict(zip(steps, routed[: replicas - 1]))

    def exchange(x, step):
        return lax.ppermute(x, "replica", [(i, i ^ step) for i in range(replicas)])

    pages = {s: exchange(send_pages[s], s) for s in steps}

    at_state, at_source, at_rank, at_order, at_ends, at_me = places(replicas, slots, count)
    planned = pl.pallas_call(
        functools.partial(plan_kernel, replicas, slots, count),
        out_shape=[shape((slots, positions, STATE), bf16)] * (replicas - 1)
        + [shape((at_me + 1,), jnp.int32)],
        in_specs=[SMEM] * 4 + [ANY],
        out_specs=[ANY] * (replicas - 1) + [SMEM],
        scratch_shapes=[
            pltpu.SMEM((replicas,), jnp.int32),
            pltpu.VMEM(read_map.shape, bf16),
            pltpu.SemaphoreType.DMA((2,)),
        ],
        compiler_params=PARAMS,
        name="plan",
    )(me, routed[-1], holder_row, cache_slot, read_map)
    plan = planned[-1]
    reads = {s: exchange(x, s) for s, x in zip(steps, planned[:-1])}
    reads[0] = read_map

    states = cache_states.reshape(cache_states.shape[0], channels, STATE)
    carried = {}
    for s in steps + [0]:
        carried[s] = pl.pallas_call(
            carried_kernel,
            out_shape=shape((slots, positions, channels), bf16),
            grid_spec=pltpu.PrefetchScalarGridSpec(
                num_scalar_prefetch=1,
                grid=(slots,),
                in_specs=[
                    pl.BlockSpec(
                        (1, positions, STATE),
                        (lambda i, plan: (i, 0, 0)) if s else (lambda i, plan: (plan[at_order + i], 0, 0)),
                    ),
                    pl.BlockSpec(
                        (1, channels, STATE), lambda i, plan, s=s: (plan[at_state + s * slots + i], 0, 0)
                    ),
                ],
                out_specs=pl.BlockSpec((1, positions, channels), lambda i, plan: (i, 0, 0)),
            ),
            compiler_params=PARAMS,
            cost_estimate=pl.CostEstimate(
                flops=2 * slots * positions * channels * STATE,
                bytes_accessed=2 * slots * channels * (STATE + positions),
                transcendentals=0,
            ),
            name="carried",
        )(plan, reads[s], states)
        if s:
            carried[s] = exchange(carried[s], s)

    spread = (jnp.arange(2 * heads)[:, None] % heads == jnp.arange(channels)[None, :] // width).astype(bf16)
    row = lambda i: (i, 0, 0)
    whole = lambda i: (0, 0)
    fixed, scaled = pl.pallas_call(
        within_kernel,
        out_shape=[shape((count, positions, channels), f32)] * 2,
        grid=(count,),
        in_specs=[
            pl.BlockSpec((1, heads), whole),
            pl.BlockSpec((1, channels), whole),
            pl.BlockSpec((2 * heads, channels), whole),
            pl.BlockSpec((1, positions, heads), row),
            pl.BlockSpec((1, positions, STATE), row),
            pl.BlockSpec((1, positions, STATE), row),
            pl.BlockSpec((1, positions, channels), row),
            pl.BlockSpec((1, positions, channels), row),
        ],
        out_specs=[pl.BlockSpec((1, positions, channels), row)] * 2,
        cost_estimate=pl.CostEstimate(
            flops=2 * count * positions * channels * positions * 8,
            bytes_accessed=count * positions * channels * 12,
            transcendentals=count * positions * channels,
        ),
        compiler_params=PARAMS,
        name="within",
    )(
        log_rates.reshape(1, heads),
        jnp.repeat(skip_gain, width).reshape(1, channels),
        spread,
        step_sizes,
        read_map,
        write_map,
        ssm_inputs,
        gate_values,
    )

    row5 = lambda i, *refs: (i, 0, 0)
    attention_output = pl.pallas_call(
        functools.partial(attention_kernel, replicas, kv_here, per_kv, page_len, most, slots),
        out_shape=shape((count, positions, queries.shape[2]), bf16),
        grid_spec=pltpu.PrefetchScalarGridSpec(
            num_scalar_prefetch=4,
            grid=(count,),
            in_specs=[
                pl.BlockSpec((1, positions, queries.shape[2]), row5),
                pl.BlockSpec((1, positions, row_width), row5),
                pl.BlockSpec((1, positions, row_width), row5),
            ]
            + [ANY] * (replicas + 1),
            out_specs=pl.BlockSpec((1, positions, queries.shape[2]), row5),
            scratch_shapes=[
                pltpu.VMEM((2, 2, most * page_len, row_width), bf16),
                pltpu.SemaphoreType.DMA((2,)),
            ],
        ),
        cost_estimate=pl.CostEstimate(
            flops=4 * count * positions * queries.shape[2] * (most * page_len + positions),
            bytes_accessed=count * (positions * queries.shape[2] * 4 + most * page_len * row_width * 4),
            transcendentals=count * positions * kv_here * per_kv * (most * page_len + positions),
        ),
        compiler_params=PARAMS,
        name="attention",
    )(
        plan,
        prefix_pages,
        suffix_length,
        page_rows,
        queries,
        suffix_keys,
        suffix_values,
        *[pages[s] for s in steps],
        page_keys,
        page_values,
    )

    mamba_output = None
    early = steps[replicas // 2 :] + [0]
    late = steps[: replicas // 2]
    for phase, members in enumerate([early, late]):

        def place(i, plan, live, phase=phase):
            first, last = span(replicas, slots, count, phase, plan)
            at = jnp.minimum(first + i, jnp.maximum(last - 1, 0))
            return (plan[at_order + at], 0, 0)

        mamba_output = pl.pallas_call(
            functools.partial(finish_kernel, replicas, slots, members, phase),
            out_shape=shape((count, positions, channels), bf16),
            grid_spec=pltpu.PrefetchScalarGridSpec(
                num_scalar_prefetch=2,
                grid=(min(count, slots * len(members)),),
                in_specs=[
                    pl.BlockSpec((1, channels), lambda i, *refs: (0, 0)),
                    pl.BlockSpec((1, positions, channels), place),
                    pl.BlockSpec((1, positions, channels), place),
                ]
                + [ANY] * (len(members) + phase),
                out_specs=pl.BlockSpec((1, positions, channels), place),
                scratch_shapes=[
                    pltpu.VMEM((2, positions, channels), bf16),
                    pltpu.SemaphoreType.DMA((2,)),
                ],
            ),
            input_output_aliases={5 + len(members): 0} if phase else {},
            cost_estimate=pl.CostEstimate(
                flops=6 * count * positions * channels,
                bytes_accessed=count * positions * channels * 6,
                transcendentals=0,
            ),
            compiler_params=PARAMS,
            name="finish",
        )(
            plan,
            suffix_length,
            norm_gain.reshape(1, channels),
            fixed,
            scaled,
            *[carried[s] for s in members],
            *([mamba_output] if phase else []),
        )
    return (mamba_output, attention_output)


def solution(mesh):
    return jax.shard_map(
        per_device,
        mesh=mesh,
        in_specs=(
            P("groups", None),
            P("groups"),
            P(("groups", "replica")),
            P("groups", None),
            P(("groups", "replica")),
            P(("groups", "replica"), "tensor", None, None),
            P(("groups", "replica"), None, "tensor"),
            P(("groups", "replica"), None, "tensor"),
            P(("groups", "replica"), None, "tensor"),
            P(("groups", "replica"), None, "tensor"),
            P("tensor"),
            P(("groups", "replica"), None, "tensor"),
            P(("groups", "replica"), None, "tensor"),
            P("tensor"),
            P(("groups", "replica"), None, "tensor"),
            P("tensor"),
            P(("groups", "replica"), None, "tensor"),
            P(("groups", "replica"), None, "tensor"),
            P(("groups", "replica"), None, "tensor"),
        ),
        out_specs=(
            P(("groups", "replica"), None, "tensor"),
            P(("groups", "replica"), None, "tensor"),
        ),
        check_vma=False,
    )
```

```python
import functools
import math

import jax
import jax.numpy as jnp
from jax import lax
from jax.experimental import pallas as pl
from jax.experimental.pallas import tpu as pltpu
from jax.sharding import PartitionSpec as P

STATE = 128
HEAD_DIM = 128
MIB = 1 << 20

ANY = pl.BlockSpec(memory_space=pl.ANY)
VMEM = pl.BlockSpec(memory_space=pltpu.VMEM)
SMEM = pl.BlockSpec(memory_space=pltpu.SMEM)
WIDE = pltpu.CompilerParams(vmem_limit_bytes=60 * MIB)
PARAMS = pltpu.CompilerParams(vmem_limit_bytes=24 * MIB)


def partner_steps(replicas):
    return list(range(replicas - 1, 0, -1))


def places(replicas, slots, count):
    state = 0
    source = state + replicas * slots
    rank = source + count
    order = rank + count
    ends = order + count
    return state, source, rank, order, ends, ends + replicas


def route_kernel(
    replicas,
    slots,
    count,
    most,
    page_len,
    me_ref,
    holder_ref,
    slot_ref,
    pages_ref,
    keys_hbm,
    values_hbm,
    reads_hbm,
    *rest,
):
    steps = partner_steps(replicas)
    read_out = dict(zip(steps, rest[: replicas - 1]))
    page_out = dict(zip(steps, rest[replicas - 1 : 2 * replicas - 2]))
    plan, keys, values, packed, seen, reads, sems = rest[2 * replicas - 2 :]
    read_sem = sems.at[replicas + 1]
    load_reads = pltpu.make_async_copy(reads_hbm, reads, sems.at[replicas + 2])
    load_reads.start()
    state, source, rank, order, ends, mine = places(replicas, slots, count)
    loads = [
        pltpu.make_async_copy(keys_hbm, keys, sems.at[0]),
        pltpu.make_async_copy(values_hbm, values, sems.at[1]),
    ]
    for load in loads:
        load.start()
    me = me_ref[0]
    plan[mine] = me

    def clear(i, carry):
        plan[state + i] = 0
        return carry

    lax.fori_loop(0, replicas * slots, clear, 0)

    def clear_seen(i, carry):
        seen[i] = 0
        return carry

    lax.fori_loop(0, replicas, clear_seen, 0)
    load_reads.wait()

    def ask(j, carry):
        step = lax.bitwise_xor(me, holder_ref[0, me * count + j])
        slot = jnp.minimum(seen[step], slots - 1)
        seen[step] = slot + 1
        plan[source + j] = step
        plan[rank + j] = slot
        for known in steps:

            @pl.when(step == known)
            def _(known=known):
                pltpu.make_async_copy(reads.at[j], read_out[known].at[slot], read_sem).start()

        return carry + (step != 0).astype(jnp.int32)

    asked = lax.fori_loop(0, count, ask, jnp.int32(0))
    for load in loads:
        load.wait()
    copies = []
    for at, step in enumerate(steps + [0]):
        first = lax.bitwise_xor(me, step) * count

        def serve(j, rank_here, at=at, step=step, first=first):
            request = first + j
            hit = holder_ref[0, request] == me

            @pl.when(hit)
            def _():
                slot = jnp.minimum(rank_here, slots - 1)
                plan[state + step * slots + slot] = slot_ref[request]
                if step:
                    for place in range(most):
                        page = pages_ref[place, request]
                        rows = slice(place * page_len, (place + 1) * page_len)
                        packed[at, slot, 0, rows, :] = keys[page]
                        packed[at, slot, 1, rows, :] = values[page]

            return rank_here + hit.astype(jnp.int32)

        lax.fori_loop(0, count, serve, jnp.int32(0))
        if step:
            copies.append(pltpu.make_async_copy(packed.at[at], page_out[step], sems.at[2 + at]))
            copies[-1].start()

    place = jnp.int32(0)
    for step in range(replicas):

        def put(j, at, step=step):
            hit = plan[source + j] == step

            @pl.when(hit)
            def _():
                plan[order + at] = j

            return at + hit.astype(jnp.int32)

        place = lax.fori_loop(0, count, put, place)
        plan[ends + step] = place

    def wait_read(i, carry):
        pltpu.make_async_copy(reads.at[0], read_out[steps[0]].at[0], read_sem).wait()
        return carry

    lax.fori_loop(0, asked, wait_read, 0)
    for copy in copies:
        copy.wait()


def carried_kernel(replicas, slots, count, steps, plan_ref, *rest):
    at_state, _, _, at_order, _, _ = places(replicas, slots, count)
    reads_hbm, states_hbm = rest[: len(steps)], rest[len(steps)]
    outs = rest[-3 - len(steps) : -3]
    reads, states, sems = rest[-3:]
    channels = states.shape[1]
    positions = reads.shape[2]
    copies = []
    for n, step in enumerate(steps):
        copies.append([])
        for k in range(slots):
            which = k if step else plan_ref[at_order + k]
            state = plan_ref[at_state + step * slots + k]
            copies[n].append(pltpu.make_async_copy(reads_hbm[n].at[which], reads.at[n, k], sems.at[n, 2 * k]))
            copies[n].append(
                pltpu.make_async_copy(
                    states_hbm.at[state],
                    states.at[n, :, k * STATE : (k + 1) * STATE],
                    sems.at[n, 2 * k + 1],
                )
            )
        for copy in copies[n]:
            copy.start()
    blank = jnp.zeros((positions, STATE), jnp.bfloat16)
    spare = STATE - slots * positions
    tile = 512
    for n in range(len(steps)):
        for copy in copies[n]:
            copy.wait()
        rows = [
            jnp.concatenate([reads[n, k] if j == k else blank for j in range(slots)], axis=1)
            for k in range(slots)
        ]
        if spare:
            rows.append(jnp.zeros((spare, slots * STATE), jnp.bfloat16))
        maps = jnp.concatenate(rows, axis=0)
        for first in range(0, channels, tile):
            product = lax.dot_general(
                states[n, first : first + tile],
                maps,
                (((1,), (1,)), ((), ())),
                preferred_element_type=jnp.float32,
            ).T.astype(jnp.bfloat16)
            for k in range(slots):
                outs[n][k, :, first : first + tile] = product[k * positions : (k + 1) * positions]


def attention_kernel(
    replicas,
    kv_here,
    per_kv,
    page_len,
    most,
    slots,
    plan_ref,
    count_ref,
    live_ref,
    pages_ref,
    query_ref,
    key_ref,
    value_ref,
    *rest,
):
    steps = partner_steps(replicas)
    arrived = dict(zip(steps, rest[: replicas - 1]))
    pool_keys, pool_values, out_ref, buffer, sems = rest[replicas - 1 :]
    i, total = pl.program_id(0), pl.num_programs(0)
    _, at_source, at_rank, _, _, at_me = places(replicas, slots, count_ref.shape[0])

    def fetch(j, slot):
        step, rank = plan_ref[at_source + j], plan_ref[at_rank + j]
        request = plan_ref[at_me] * count_ref.shape[0] + j
        for known in steps:

            @pl.when(step == known)
            def _(known=known):
                pltpu.make_async_copy(arrived[known].at[rank], buffer.at[slot], sems.at[slot]).start()

        @pl.when(step == 0)
        def _():
            for place in range(most):
                page = pages_ref[place, request]
                rows = pl.ds(place * page_len, page_len)
                pltpu.make_async_copy(pool_keys.at[page], buffer.at[slot, 0, rows], sems.at[slot]).start()
                pltpu.make_async_copy(pool_values.at[page], buffer.at[slot, 1, rows], sems.at[slot]).start()

    @pl.when(i == 0)
    def _():
        fetch(i, 0)

    @pl.when(i + 1 < total)
    def _():
        fetch(i + 1, lax.rem(i + 1, 2))

    now = lax.rem(i, 2)
    pltpu.make_async_copy(buffer.at[now], buffer.at[now], sems.at[now]).wait()

    positions = query_ref.shape[1]
    rows = per_kv * positions
    cached = most * page_len
    live = live_ref[i]
    scale = 1.0 / math.sqrt(HEAD_DIM)
    column = lax.broadcasted_iota(jnp.int32, (rows, cached), 1)
    ahead = column < count_ref[i] * page_len
    row = lax.broadcasted_iota(jnp.int32, (rows, positions), 0) & (positions - 1)
    causal = lax.broadcasted_iota(jnp.int32, (rows, positions), 1) <= row
    alive = (lax.broadcasted_iota(jnp.int32, (rows, HEAD_DIM), 0) & (positions - 1)) < live
    contract = (((1,), (1,)), ((), ()))
    for g in range(kv_here):
        lanes = slice(g * HEAD_DIM, (g + 1) * HEAD_DIM)
        heads = [(g * per_kv + q) * HEAD_DIM for q in range(per_kv)]
        query = jnp.concatenate([query_ref[0, :, h : h + HEAD_DIM] for h in heads], axis=0)
        old_keys, old_values = buffer[now, 0, :, lanes], buffer[now, 1, :, lanes]
        new_keys, new_values = key_ref[0, :, lanes], value_ref[0, :, lanes]
        old = lax.dot_general(query, old_keys, contract, preferred_element_type=jnp.float32) * scale
        new = lax.dot_general(query, new_keys, contract, preferred_element_type=jnp.float32) * scale
        old = jnp.where(ahead, old, -1e30)
        new = jnp.where(causal, new, -1e30)
        top = jnp.maximum(jnp.max(old, axis=1, keepdims=True), jnp.max(new, axis=1, keepdims=True))
        old, new = jnp.exp(old - top), jnp.exp(new - top)
        share = 1.0 / (jnp.sum(old, axis=1, keepdims=True) + jnp.sum(new, axis=1, keepdims=True))
        old, new = (old * share).astype(jnp.bfloat16), (new * share).astype(jnp.bfloat16)
        result = jnp.dot(old, old_values, preferred_element_type=jnp.float32) + jnp.dot(
            new, new_values, preferred_element_type=jnp.float32
        )
        result = jnp.where(alive, result, 0.0).astype(out_ref.dtype)
        for q, h in enumerate(heads):
            out_ref[0, :, h : h + HEAD_DIM] = result[q * positions : (q + 1) * positions]


def halves(x):
    high = x.astype(jnp.bfloat16)
    return high, (x - high.astype(jnp.float32)).astype(jnp.bfloat16)


def within_kernel(
    rate_ref, skip_ref, spread_ref, step_ref, read_ref, write_ref, input_ref, gate_ref, fixed_ref, scaled_ref
):
    positions = input_ref.shape[1]
    heads = step_ref.shape[2]
    step = step_ref[0]
    later = lax.broadcasted_iota(jnp.int32, (positions, positions), 0)
    earlier = lax.broadcasted_iota(jnp.int32, (positions, positions), 1)
    causal = earlier <= later
    decays = step * (-jnp.exp(rate_ref[...]))
    running = lax.dot_general(
        causal.astype(jnp.float32),
        decays,
        (((1,), (0,)), ((), ())),
        precision=lax.Precision.HIGHEST,
        preferred_element_type=jnp.float32,
    )
    decay = jnp.exp(running)
    growth = jnp.exp(-running) * step
    both = jnp.concatenate([decay, growth], axis=0)
    high, low = halves(both)
    wide = jnp.dot(
        jnp.concatenate([high, low], axis=1), spread_ref[...], preferred_element_type=jnp.float32
    )
    decay, growth = wide[:positions], wide[positions:]
    contact = lax.dot_general(
        read_ref[0], write_ref[0], (((1,), (1,)), ((), ())), preferred_element_type=jnp.float32
    )
    contact = jnp.where(causal, contact, 0.0)
    contact_high, contact_low = halves(contact)
    inputs = input_ref[0].astype(jnp.float32)
    weighed = (inputs * growth).astype(jnp.bfloat16)
    within = jnp.dot(
        jnp.concatenate([contact_high, contact_low], axis=1),
        jnp.concatenate([weighed, weighed], axis=0),
        preferred_element_type=jnp.float32,
    )
    gate = gate_ref[0].astype(jnp.float32)
    gate = gate / (1.0 + jnp.exp(-gate))
    fixed_ref[0] = gate * (decay * within + skip_ref[...] * inputs)
    scaled_ref[0] = gate * decay


def finish_kernel(
    replicas, slots, members, chained, plan_ref, live_ref, gain_ref, fixed_ref, scaled_ref, *rest
):
    count = live_ref.shape[0]
    _, at_source, at_rank, at_order, at_ends, _ = places(replicas, slots, count)
    arrived = dict(zip(members, rest[: len(members)]))
    out_ref, ready, sem = rest[len(members) + chained :]
    positions, channels = fixed_ref.shape[1:]
    first = plan_ref[at_ends + members[0] - 1] if members[0] else 0
    last = plan_ref[at_ends + members[-1]]

    def copy(i):
        request = plan_ref[at_order + i]
        return pltpu.make_async_copy(ready.at[request], out_ref.at[request], sem)

    def finish(i, carry):
        request = plan_ref[at_order + i]
        alive = lax.broadcasted_iota(jnp.int32, (positions, 1), 0) < live_ref[request]
        for known in members:

            @pl.when(plan_ref[at_source + request] == known)
            def _(known=known):
                carried = arrived[known][plan_ref[at_rank + request]].astype(jnp.float32)
                gated = fixed_ref[request] + scaled_ref[request] * carried
                square = jnp.sum(gated * gated, axis=1, keepdims=True) * (1.0 / channels)
                factor = jnp.where(alive, lax.rsqrt(square + 1e-05), 0.0)
                ready[request] = (gated * factor * gain_ref[...]).astype(out_ref.dtype)

        copy(i).start()
        return carry

    lax.fori_loop(first, last, finish, 0)

    def wait(i, carry):
        copy(i).wait()
        return carry

    lax.fori_loop(first, last, wait, 0)


def per_device(
    holder,
    cache_slot,
    prefix_pages,
    page_ids,
    suffix_length,
    cache_states,
    page_keys,
    page_values,
    ssm_inputs,
    step_sizes,
    log_rates,
    write_map,
    read_map,
    skip_gain,
    gate_values,
    norm_gain,
    queries,
    suffix_keys,
    suffix_values,
):
    replicas = lax.axis_size("replica")
    assert replicas & (replicas - 1) == 0
    myself = lax.axis_index("replica").astype(jnp.int32)
    count, positions, channels = ssm_inputs.shape
    slots = (count + replicas - 1) // replicas
    heads = log_rates.shape[0]
    width = channels // heads
    assert write_map.shape[2] == STATE
    page_len, row_width = page_keys.shape[1:]
    most = page_ids.shape[1]
    kv_here = row_width // HEAD_DIM
    per_kv = queries.shape[2] // row_width
    bf16, f32 = jnp.bfloat16, jnp.float32
    steps = partner_steps(replicas)
    shape = jax.ShapeDtypeStruct

    me = myself.reshape(1)
    holder_row = holder.T
    page_rows = page_ids.T
    def exchange(x, step):
        return lax.ppermute(x, "replica", [(i, i ^ step) for i in range(replicas)])

    at_state, at_source, at_rank, at_order, at_ends, at_me = places(replicas, slots, count)
    routed = pl.pallas_call(
        functools.partial(route_kernel, replicas, slots, count, most, page_len),
        out_shape=[shape((slots, positions, STATE), bf16)] * (replicas - 1)
        + [shape((slots, 2, most * page_len, row_width), bf16)] * (replicas - 1)
        + [shape((at_me + 1,), jnp.int32)],
        in_specs=[SMEM] * 4 + [ANY] * 3,
        out_specs=[ANY] * (2 * replicas - 2) + [SMEM],
        scratch_shapes=[
            pltpu.VMEM(page_keys.shape, bf16),
            pltpu.VMEM(page_values.shape, bf16),
            pltpu.VMEM((replicas - 1, slots, 2, most * page_len, row_width), bf16),
            pltpu.SMEM((replicas,), jnp.int32),
            pltpu.VMEM(read_map.shape, bf16),
            pltpu.SemaphoreType.DMA((replicas + 3,)),
        ],
        compiler_params=WIDE,
        name="route",
    )(me, holder_row, cache_slot, page_rows, page_keys, page_values, read_map)
    reads = {s: exchange(x, s) for s, x in zip(steps, routed[: replicas - 1])}
    reads[0] = read_map
    pages = {s: exchange(x, s) for s, x in zip(steps, routed[replicas - 1 : -1])}
    plan = routed[-1]

    states = cache_states.reshape(cache_states.shape[0], channels, STATE)
    carried = {}
    token = []
    half = max(1, replicas // 2)
    for served in (steps + [0],):
        results = pl.pallas_call(
            functools.partial(carried_kernel, replicas, slots, count, served),
            out_shape=[shape((slots, positions, channels), bf16)] * len(served),
            grid_spec=pltpu.PrefetchScalarGridSpec(
                num_scalar_prefetch=1,
                grid=(1,),
                in_specs=[ANY] * (len(served) + 1 + len(token)),
                out_specs=[pl.BlockSpec((slots, positions, channels), lambda i, plan: (0, 0, 0))] * len(served),
                scratch_shapes=[
                    pltpu.VMEM((len(served), slots, positions, STATE), bf16),
                    pltpu.VMEM((len(served), channels, slots * STATE), bf16),
                    pltpu.SemaphoreType.DMA((len(served), 2 * slots)),
                ],
            ),
            compiler_params=WIDE,
            cost_estimate=pl.CostEstimate(
                flops=64 * len(served) * slots * positions * channels * STATE,
                bytes_accessed=2 * len(served) * slots * channels * (STATE + positions),
                transcendentals=0,
            ),
            name="carried",
        )(plan, *[reads[s] for s in served], states, *token)
        token = [results[0]]
        for s, x in zip(served, results):
            carried[s] = exchange(x, s) if s else x

    spread = (jnp.arange(2 * heads)[:, None] % heads == jnp.arange(channels)[None, :] // width).astype(bf16)
    skip_wide = jnp.repeat(skip_gain, width).reshape(1, channels)
    row = lambda i: (i, 0, 0)
    whole = lambda i: (0, 0)
    fixed, scaled = pl.pallas_call(
        within_kernel,
        out_shape=[shape((count, positions, channels), f32)] * 2,
        grid=(count,),
        in_specs=[
            pl.BlockSpec((1, heads), whole),
            pl.BlockSpec((1, channels), whole),
            pl.BlockSpec((2 * heads, channels), whole),
            pl.BlockSpec((1, positions, heads), row),
            pl.BlockSpec((1, positions, STATE), row),
            pl.BlockSpec((1, positions, STATE), row),
            pl.BlockSpec((1, positions, channels), row),
            pl.BlockSpec((1, positions, channels), row),
        ],
        out_specs=[pl.BlockSpec((1, positions, channels), row)] * 2,
        cost_estimate=pl.CostEstimate(
            flops=2 * count * positions * channels * positions * 8,
            bytes_accessed=count * positions * channels * 12,
            transcendentals=count * positions * channels,
        ),
        compiler_params=PARAMS,
        name="within",
    )(
        log_rates.reshape(1, heads),
        skip_wide,
        spread,
        step_sizes,
        read_map,
        write_map,
        ssm_inputs,
        gate_values,
    )

    row5 = lambda i, *refs: (i, 0, 0)
    attention_output = pl.pallas_call(
        functools.partial(attention_kernel, replicas, kv_here, per_kv, page_len, most, slots),
        out_shape=shape((count, positions, queries.shape[2]), bf16),
        grid_spec=pltpu.PrefetchScalarGridSpec(
            num_scalar_prefetch=4,
            grid=(count,),
            in_specs=[
                pl.BlockSpec((1, positions, queries.shape[2]), row5),
                pl.BlockSpec((1, positions, row_width), row5),
                pl.BlockSpec((1, positions, row_width), row5),
            ]
            + [ANY] * (replicas + 1),
            out_specs=pl.BlockSpec((1, positions, queries.shape[2]), row5),
            scratch_shapes=[
                pltpu.VMEM((2, 2, most * page_len, row_width), bf16),
                pltpu.SemaphoreType.DMA((2,)),
            ],
        ),
        cost_estimate=pl.CostEstimate(
            flops=4 * count * positions * queries.shape[2] * (most * page_len + positions),
            bytes_accessed=count * (positions * queries.shape[2] * 4 + most * page_len * row_width * 4),
            transcendentals=count * positions * kv_here * per_kv * (most * page_len + positions),
        ),
        compiler_params=PARAMS,
        name="attention",
    )(
        plan,
        prefix_pages,
        suffix_length,
        page_rows,
        queries,
        suffix_keys,
        suffix_values,
        *[pages[s] for s in steps],
        page_keys,
        page_values,
    )

    mamba_output = None
    for members in (list(range(half)), list(range(half, replicas))):
        chained = 0 if mamba_output is None else 1
        mamba_output = pl.pallas_call(
            functools.partial(finish_kernel, replicas, slots, members, chained),
            out_shape=shape((count, positions, channels), bf16),
            in_specs=[SMEM] * 2 + [VMEM] * (3 + len(members)) + [ANY] * chained,
            out_specs=ANY,
            scratch_shapes=[pltpu.VMEM((count, positions, channels), bf16), pltpu.SemaphoreType.DMA],
            input_output_aliases={5 + len(members): 0} if chained else {},
            compiler_params=PARAMS,
            cost_estimate=pl.CostEstimate(
                flops=len(members) * slots * positions * channels * 8,
                bytes_accessed=len(members) * slots * positions * channels * 12,
                transcendentals=0,
            ),
            name="finish",
        )(
            plan,
            suffix_length,
            norm_gain.reshape(1, channels),
            fixed,
            scaled,
            *[carried[s] for s in members],
            *([mamba_output] if chained else []),
        )
    return (mamba_output, attention_output)


def solution(mesh):
    return jax.shard_map(
        per_device,
        mesh=mesh,
        in_specs=(
            P("groups", None),
            P("groups"),
            P(("groups", "replica")),
            P("groups", None),
            P(("groups", "replica")),
            P(("groups", "replica"), "tensor", None, None),
            P(("groups", "replica"), None, "tensor"),
            P(("groups", "replica"), None, "tensor"),
            P(("groups", "replica"), None, "tensor"),
            P(("groups", "replica"), None, "tensor"),
            P("tensor"),
            P(("groups", "replica"), None, "tensor"),
            P(("groups", "replica"), None, "tensor"),
            P("tensor"),
            P(("groups", "replica"), None, "tensor"),
            P("tensor"),
            P(("groups", "replica"), None, "tensor"),
            P(("groups", "replica"), None, "tensor"),
            P(("groups", "replica"), None, "tensor"),
        ),
        out_specs=(
            P(("groups", "replica"), None, "tensor"),
            P(("groups", "replica"), None, "tensor"),
        ),
        check_vma=False,
    )
```

```python
import functools
import math

import jax
import jax.numpy as jnp
from jax import lax
from jax.experimental import pallas as pl
from jax.experimental.pallas import tpu as pltpu
from jax.sharding import PartitionSpec as P

STATE = 128
HEAD_DIM = 128
MIB = 1 << 20

ANY = pl.BlockSpec(memory_space=pl.ANY)
VMEM = pl.BlockSpec(memory_space=pltpu.VMEM)
SMEM = pl.BlockSpec(memory_space=pltpu.SMEM)
WIDE = pltpu.CompilerParams(vmem_limit_bytes=60 * MIB)
PARAMS = pltpu.CompilerParams(vmem_limit_bytes=24 * MIB)


def partner_steps(replicas):
    return list(range(replicas - 1, 0, -1))


def places(replicas, slots, count):
    state = 0
    source = state + replicas * slots
    rank = source + count
    order = rank + count
    ends = order + count
    return state, source, rank, order, ends, ends + replicas


def pack_pages(replicas, slots, count, most, page_len, steps, me, holder_ref, pages_ref, pools, packed, outs, sems):
    keys, values = pools
    copies = []
    for at, step in enumerate(steps):
        first = lax.bitwise_xor(me, step) * count

        def serve(j, rank_here, at=at, first=first):
            request = first + j
            hit = holder_ref[0, request] == me

            @pl.when(hit)
            def _():
                slot = jnp.minimum(rank_here, slots - 1)
                for place in range(most):
                    page = pages_ref[place, request]
                    rows = slice(place * page_len, (place + 1) * page_len)
                    packed[at, slot, 0, rows, :] = keys[page]
                    packed[at, slot, 1, rows, :] = values[page]

            return rank_here + hit.astype(jnp.int32)

        lax.fori_loop(0, count, serve, jnp.int32(0))
        copies.append(pltpu.make_async_copy(packed.at[at], outs[at], sems.at[at]))
        copies[-1].start()
    return copies


def clear(ref, length):
    def body(i, carry):
        ref[i] = 0
        return carry

    lax.fori_loop(0, length, body, 0)


def first_kernel(
    replicas,
    slots,
    count,
    most,
    page_len,
    far,
    me_ref,
    holder_ref,
    pages_ref,
    keys_hbm,
    values_hbm,
    reads_hbm,
    *rest,
):
    steps = partner_steps(replicas)
    page_out, rest = rest[: len(far)], rest[len(far) :]
    read_out, rest = dict(zip(steps, rest[: replicas - 1])), rest[replicas - 1 :]
    keys, values, packed, seen, reads, sems, page_sems = rest
    loads = [
        pltpu.make_async_copy(keys_hbm, keys, sems.at[0]),
        pltpu.make_async_copy(values_hbm, values, sems.at[1]),
        pltpu.make_async_copy(reads_hbm, reads, sems.at[2]),
    ]
    for load in loads:
        load.start()
    me = me_ref[0]
    clear(seen, replicas)
    for load in loads:
        load.wait()
    copies = pack_pages(
        replicas, slots, count, most, page_len, far, me, holder_ref, pages_ref, (keys, values), packed, page_out, page_sems
    )

    def ask(j, sent):
        step = lax.bitwise_xor(me, holder_ref[0, me * count + j])
        slot = jnp.minimum(seen[step], slots - 1)
        seen[step] = slot + 1
        for known in steps:

            @pl.when(step == known)
            def _(known=known):
                pltpu.make_async_copy(reads.at[j], read_out[known].at[slot], sems.at[3]).start()

        return sent + (step != 0).astype(jnp.int32)

    sent = lax.fori_loop(0, count, ask, jnp.int32(0))

    def wait_read(i, carry):
        pltpu.make_async_copy(reads.at[0], read_out[steps[0]].at[0], sems.at[3]).wait()
        return carry

    lax.fori_loop(0, sent, wait_read, 0)
    for copy in copies:
        copy.wait()


def second_kernel(
    replicas,
    slots,
    count,
    most,
    page_len,
    near,
    waited,
    me_ref,
    holder_ref,
    slot_ref,
    pages_ref,
    keys_hbm,
    values_hbm,
    *rest,
):
    page_out = rest[waited : waited + len(near)]
    plan, keys, values, packed, seen, sems, page_sems = rest[waited + len(near) :]
    state, source, rank, order, ends, mine = places(replicas, slots, count)
    loads = [
        pltpu.make_async_copy(keys_hbm, keys, sems.at[0]),
        pltpu.make_async_copy(values_hbm, values, sems.at[1]),
    ]
    for load in loads:
        load.start()
    me = me_ref[0]
    plan[mine] = me
    clear(plan, replicas * slots)
    clear(seen, replicas)
    for load in loads:
        load.wait()
    copies = pack_pages(
        replicas, slots, count, most, page_len, near, me, holder_ref, pages_ref, (keys, values), packed, page_out, page_sems
    )
    for step in range(replicas):
        first = lax.bitwise_xor(me, step) * count

        def serve(j, rank_here, step=step, first=first):
            hit = holder_ref[0, first + j] == me

            @pl.when(hit)
            def _():
                plan[state + step * slots + jnp.minimum(rank_here, slots - 1)] = slot_ref[first + j]

            return rank_here + hit.astype(jnp.int32)

        lax.fori_loop(0, count, serve, jnp.int32(0))

    def ask(j, carry):
        step = lax.bitwise_xor(me, holder_ref[0, me * count + j])
        slot = jnp.minimum(seen[step], slots - 1)
        seen[step] = slot + 1
        plan[source + j] = step
        plan[rank + j] = slot
        return carry

    lax.fori_loop(0, count, ask, 0)
    place = jnp.int32(0)
    for step in range(replicas):

        def put(j, at, step=step):
            hit = plan[source + j] == step

            @pl.when(hit)
            def _():
                plan[order + at] = j

            return at + hit.astype(jnp.int32)

        place = lax.fori_loop(0, count, put, place)
        plan[ends + step] = place
    for copy in copies:
        copy.wait()


def carried_kernel(replicas, slots, count, steps, plan_ref, *rest):
    at_state, _, _, at_order, _, _ = places(replicas, slots, count)
    reads_hbm, states_hbm = rest[: len(steps)], rest[len(steps)]
    outs = rest[-3 - len(steps) : -3]
    reads, states, sems = rest[-3:]
    channels = states.shape[1]
    positions = reads.shape[2]
    copies = []
    for n, step in enumerate(steps):
        copies.append([])
        for k in range(slots):
            which = k if step else plan_ref[at_order + k]
            state = plan_ref[at_state + step * slots + k]
            copies[n].append(pltpu.make_async_copy(reads_hbm[n].at[which], reads.at[n, k], sems.at[n, 2 * k]))
            copies[n].append(
                pltpu.make_async_copy(
                    states_hbm.at[state],
                    states.at[n, :, k * STATE : (k + 1) * STATE],
                    sems.at[n, 2 * k + 1],
                )
            )
        for copy in copies[n]:
            copy.start()
    blank = jnp.zeros((positions, STATE), jnp.bfloat16)
    spare = STATE - slots * positions
    tile = 512
    for n in range(len(steps)):
        for copy in copies[n]:
            copy.wait()
        rows = [
            jnp.concatenate([reads[n, k] if j == k else blank for j in range(slots)], axis=1)
            for k in range(slots)
        ]
        if spare:
            rows.append(jnp.zeros((spare, slots * STATE), jnp.bfloat16))
        maps = jnp.concatenate(rows, axis=0)
        for first in range(0, channels, tile):
            product = lax.dot_general(
                states[n, first : first + tile],
                maps,
                (((1,), (1,)), ((), ())),
                preferred_element_type=jnp.float32,
            ).T.astype(jnp.bfloat16)
            for k in range(slots):
                outs[n][k, :, first : first + tile] = product[k * positions : (k + 1) * positions]


def attention_kernel(
    replicas,
    kv_here,
    per_kv,
    page_len,
    most,
    slots,
    plan_ref,
    count_ref,
    live_ref,
    pages_ref,
    query_ref,
    key_ref,
    value_ref,
    *rest,
):
    steps = partner_steps(replicas)
    arrived = dict(zip(steps, rest[: replicas - 1]))
    pool_keys, pool_values, out_ref, buffer, sems = rest[replicas - 1 :]
    i, total = pl.program_id(0), pl.num_programs(0)
    _, at_source, at_rank, _, _, at_me = places(replicas, slots, count_ref.shape[0])

    def fetch(j, slot):
        step, rank = plan_ref[at_source + j], plan_ref[at_rank + j]
        request = plan_ref[at_me] * count_ref.shape[0] + j
        for known in steps:

            @pl.when(step == known)
            def _(known=known):
                pltpu.make_async_copy(arrived[known].at[rank], buffer.at[slot], sems.at[slot]).start()

        @pl.when(step == 0)
        def _():
            for place in range(most):
                page = pages_ref[place, request]
                rows = pl.ds(place * page_len, page_len)
                pltpu.make_async_copy(pool_keys.at[page], buffer.at[slot, 0, rows], sems.at[slot]).start()
                pltpu.make_async_copy(pool_values.at[page], buffer.at[slot, 1, rows], sems.at[slot]).start()

    @pl.when(i == 0)
    def _():
        fetch(i, 0)

    @pl.when(i + 1 < total)
    def _():
        fetch(i + 1, lax.rem(i + 1, 2))

    now = lax.rem(i, 2)
    pltpu.make_async_copy(buffer.at[now], buffer.at[now], sems.at[now]).wait()

    positions = query_ref.shape[1]
    rows = per_kv * positions
    cached = most * page_len
    live = live_ref[i]
    scale = 1.0 / math.sqrt(HEAD_DIM)
    column = lax.broadcasted_iota(jnp.int32, (rows, cached), 1)
    ahead = column < count_ref[i] * page_len
    row = lax.broadcasted_iota(jnp.int32, (rows, positions), 0) & (positions - 1)
    causal = lax.broadcasted_iota(jnp.int32, (rows, positions), 1) <= row
    alive = (lax.broadcasted_iota(jnp.int32, (rows, HEAD_DIM), 0) & (positions - 1)) < live
    contract = (((1,), (1,)), ((), ()))
    for g in range(kv_here):
        lanes = slice(g * HEAD_DIM, (g + 1) * HEAD_DIM)
        heads = [(g * per_kv + q) * HEAD_DIM for q in range(per_kv)]
        query = jnp.concatenate([query_ref[0, :, h : h + HEAD_DIM] for h in heads], axis=0)
        old_keys, old_values = buffer[now, 0, :, lanes], buffer[now, 1, :, lanes]
        new_keys, new_values = key_ref[0, :, lanes], value_ref[0, :, lanes]
        old = lax.dot_general(query, old_keys, contract, preferred_element_type=jnp.float32) * scale
        new = lax.dot_general(query, new_keys, contract, preferred_element_type=jnp.float32) * scale
        old = jnp.where(ahead, old, -1e30)
        new = jnp.where(causal, new, -1e30)
        top = jnp.maximum(jnp.max(old, axis=1, keepdims=True), jnp.max(new, axis=1, keepdims=True))
        old, new = jnp.exp(old - top), jnp.exp(new - top)
        share = 1.0 / (jnp.sum(old, axis=1, keepdims=True) + jnp.sum(new, axis=1, keepdims=True))
        old, new = (old * share).astype(jnp.bfloat16), (new * share).astype(jnp.bfloat16)
        result = jnp.dot(old, old_values, preferred_element_type=jnp.float32) + jnp.dot(
            new, new_values, preferred_element_type=jnp.float32
        )
        result = jnp.where(alive, result, 0.0).astype(out_ref.dtype)
        for q, h in enumerate(heads):
            out_ref[0, :, h : h + HEAD_DIM] = result[q * positions : (q + 1) * positions]


def halves(x):
    high = x.astype(jnp.bfloat16)
    return high, (x - high.astype(jnp.float32)).astype(jnp.bfloat16)


def within_kernel(
    rate_ref, skip_ref, spread_ref, step_ref, read_ref, write_ref, input_ref, gate_ref, fixed_ref, scaled_ref
):
    positions = input_ref.shape[1]
    heads = step_ref.shape[2]
    step = step_ref[0]
    later = lax.broadcasted_iota(jnp.int32, (positions, positions), 0)
    earlier = lax.broadcasted_iota(jnp.int32, (positions, positions), 1)
    causal = earlier <= later
    decays = step * (-jnp.exp(rate_ref[...]))
    running = lax.dot_general(
        causal.astype(jnp.float32),
        decays,
        (((1,), (0,)), ((), ())),
        precision=lax.Precision.HIGHEST,
        preferred_element_type=jnp.float32,
    )
    decay = jnp.exp(running)
    growth = jnp.exp(-running) * step
    both = jnp.concatenate([decay, growth], axis=0)
    high, low = halves(both)
    wide = jnp.dot(
        jnp.concatenate([high, low], axis=1), spread_ref[...], preferred_element_type=jnp.float32
    )
    decay, growth = wide[:positions], wide[positions:]
    contact = lax.dot_general(
        read_ref[0], write_ref[0], (((1,), (1,)), ((), ())), preferred_element_type=jnp.float32
    )
    contact = jnp.where(causal, contact, 0.0)
    contact_high, contact_low = halves(contact)
    inputs = input_ref[0].astype(jnp.float32)
    weighed = (inputs * growth).astype(jnp.bfloat16)
    within = jnp.dot(
        jnp.concatenate([contact_high, contact_low], axis=1),
        jnp.concatenate([weighed, weighed], axis=0),
        preferred_element_type=jnp.float32,
    )
    gate = gate_ref[0].astype(jnp.float32)
    gate = gate / (1.0 + jnp.exp(-gate))
    fixed_ref[0] = gate * (decay * within + skip_ref[...] * inputs)
    scaled_ref[0] = gate * decay


def finish_kernel(
    replicas, slots, members, chained, plan_ref, live_ref, gain_ref, fixed_ref, scaled_ref, *rest
):
    count = live_ref.shape[0]
    _, at_source, at_rank, at_order, at_ends, _ = places(replicas, slots, count)
    arrived = dict(zip(members, rest[: len(members)]))
    out_ref, ready, sem = rest[len(members) + chained :]
    positions, channels = fixed_ref.shape[1:]
    first = plan_ref[at_ends + members[0] - 1] if members[0] else 0
    last = plan_ref[at_ends + members[-1]]

    def copy(i):
        request = plan_ref[at_order + i]
        return pltpu.make_async_copy(ready.at[request], out_ref.at[request], sem)

    def finish(i, carry):
        request = plan_ref[at_order + i]
        alive = lax.broadcasted_iota(jnp.int32, (positions, 1), 0) < live_ref[request]
        for known in members:

            @pl.when(plan_ref[at_source + request] == known)
            def _(known=known):
                carried = arrived[known][plan_ref[at_rank + request]].astype(jnp.float32)
                gated = fixed_ref[request] + scaled_ref[request] * carried
                square = jnp.sum(gated * gated, axis=1, keepdims=True) * (1.0 / channels)
                factor = jnp.where(alive, lax.rsqrt(square + 1e-05), 0.0)
                ready[request] = (gated * factor * gain_ref[...]).astype(out_ref.dtype)

        copy(i).start()
        return carry

    lax.fori_loop(first, last, finish, 0)

    def wait(i, carry):
        copy(i).wait()
        return carry

    lax.fori_loop(first, last, wait, 0)


def per_device(
    holder,
    cache_slot,
    prefix_pages,
    page_ids,
    suffix_length,
    cache_states,
    page_keys,
    page_values,
    ssm_inputs,
    step_sizes,
    log_rates,
    write_map,
    read_map,
    skip_gain,
    gate_values,
    norm_gain,
    queries,
    suffix_keys,
    suffix_values,
):
    replicas = lax.axis_size("replica")
    assert replicas & (replicas - 1) == 0
    myself = lax.axis_index("replica").astype(jnp.int32)
    count, positions, channels = ssm_inputs.shape
    slots = (count + replicas - 1) // replicas
    heads = log_rates.shape[0]
    width = channels // heads
    assert write_map.shape[2] == STATE
    page_len, row_width = page_keys.shape[1:]
    most = page_ids.shape[1]
    kv_here = row_width // HEAD_DIM
    per_kv = queries.shape[2] // row_width
    bf16, f32 = jnp.bfloat16, jnp.float32
    steps = partner_steps(replicas)
    shape = jax.ShapeDtypeStruct

    me = myself.reshape(1)
    holder_row = holder.T
    page_rows = page_ids.T
    def exchange(x, step):
        return lax.ppermute(x, "replica", [(i, i ^ step) for i in range(replicas)])

    at_state, at_source, at_rank, at_order, at_ends, at_me = places(replicas, slots, count)
    third = max(1, (replicas - 1) // 3)
    far, near = steps[:third], steps[third:]
    page_shape = shape((slots, 2, most * page_len, row_width), bf16)
    first = pl.pallas_call(
        functools.partial(first_kernel, replicas, slots, count, most, page_len, far),
        out_shape=[page_shape] * len(far) + [shape((slots, positions, STATE), bf16)] * (replicas - 1),
        in_specs=[SMEM] * 3 + [ANY] * 3,
        out_specs=[ANY] * (len(far) + replicas - 1),
        scratch_shapes=[
            pltpu.VMEM(page_keys.shape, bf16),
            pltpu.VMEM(page_values.shape, bf16),
            pltpu.VMEM((len(far), *page_shape.shape), bf16),
            pltpu.SMEM((replicas,), jnp.int32),
            pltpu.VMEM(read_map.shape, bf16),
            pltpu.SemaphoreType.DMA((4,)),
            pltpu.SemaphoreType.DMA((len(far),)),
        ],
        compiler_params=WIDE,
        name="first",
    )(me, holder_row, page_rows, page_keys, page_values, read_map)
    pages = {s: exchange(x, s) for s, x in zip(far, first)}
    reads = {s: exchange(x, s) for s, x in zip(steps, first[len(far) :])}
    waited = []
    second = pl.pallas_call(
        functools.partial(second_kernel, replicas, slots, count, most, page_len, near, len(waited)),
        out_shape=[page_shape] * len(near) + [shape((at_me + 1,), jnp.int32)],
        in_specs=[SMEM] * 4 + [ANY] * (2 + len(waited)),
        out_specs=[ANY] * len(near) + [SMEM],
        scratch_shapes=[
            pltpu.VMEM(page_keys.shape, bf16),
            pltpu.VMEM(page_values.shape, bf16),
            pltpu.VMEM((len(near), *page_shape.shape), bf16),
            pltpu.SMEM((replicas,), jnp.int32),
            pltpu.SemaphoreType.DMA((2,)),
            pltpu.SemaphoreType.DMA((len(near),)),
        ],
        compiler_params=WIDE,
        name="second",
    )(me, holder_row, cache_slot, page_rows, page_keys, page_values, *waited)
    pages.update({s: exchange(x, s) for s, x in zip(near, second[:-1])})
    reads[0] = read_map
    plan = second[-1]

    states = cache_states.reshape(cache_states.shape[0], channels, STATE)
    carried = {}
    token = []
    half = max(1, replicas // 2)
    for served in (steps + [0],):
        results = pl.pallas_call(
            functools.partial(carried_kernel, replicas, slots, count, served),
            out_shape=[shape((slots, positions, channels), bf16)] * len(served),
            grid_spec=pltpu.PrefetchScalarGridSpec(
                num_scalar_prefetch=1,
                grid=(1,),
                in_specs=[ANY] * (len(served) + 1 + len(token)),
                out_specs=[pl.BlockSpec((slots, positions, channels), lambda i, plan: (0, 0, 0))] * len(served),
                scratch_shapes=[
                    pltpu.VMEM((len(served), slots, positions, STATE), bf16),
                    pltpu.VMEM((len(served), channels, slots * STATE), bf16),
                    pltpu.SemaphoreType.DMA((len(served), 2 * slots)),
                ],
            ),
            compiler_params=WIDE,
            cost_estimate=pl.CostEstimate(
                flops=64 * len(served) * slots * positions * channels * STATE,
                bytes_accessed=2 * len(served) * slots * channels * (STATE + positions),
                transcendentals=0,
            ),
            name="carried",
        )(plan, *[reads[s] for s in served], states, *token)
        token = [results[0]]
        for s, x in zip(served, results):
            carried[s] = exchange(x, s) if s else x

    spread = (jnp.arange(2 * heads)[:, None] % heads == jnp.arange(channels)[None, :] // width).astype(bf16)
    skip_wide = jnp.repeat(skip_gain, width).reshape(1, channels)
    row = lambda i: (i, 0, 0)
    whole = lambda i: (0, 0)
    fixed, scaled = pl.pallas_call(
        within_kernel,
        out_shape=[shape((count, positions, channels), f32)] * 2,
        grid=(count,),
        in_specs=[
            pl.BlockSpec((1, heads), whole),
            pl.BlockSpec((1, channels), whole),
            pl.BlockSpec((2 * heads, channels), whole),
            pl.BlockSpec((1, positions, heads), row),
            pl.BlockSpec((1, positions, STATE), row),
            pl.BlockSpec((1, positions, STATE), row),
            pl.BlockSpec((1, positions, channels), row),
            pl.BlockSpec((1, positions, channels), row),
        ],
        out_specs=[pl.BlockSpec((1, positions, channels), row)] * 2,
        cost_estimate=pl.CostEstimate(
            flops=2 * count * positions * channels * positions * 8,
            bytes_accessed=count * positions * channels * 12,
            transcendentals=count * positions * channels,
        ),
        compiler_params=PARAMS,
        name="within",
    )(
        log_rates.reshape(1, heads),
        skip_wide,
        spread,
        step_sizes,
        read_map,
        write_map,
        ssm_inputs,
        gate_values,
    )

    row5 = lambda i, *refs: (i, 0, 0)
    attention_output = pl.pallas_call(
        functools.partial(attention_kernel, replicas, kv_here, per_kv, page_len, most, slots),
        out_shape=shape((count, positions, queries.shape[2]), bf16),
        grid_spec=pltpu.PrefetchScalarGridSpec(
            num_scalar_prefetch=4,
            grid=(count,),
            in_specs=[
                pl.BlockSpec((1, positions, queries.shape[2]), row5),
                pl.BlockSpec((1, positions, row_width), row5),
                pl.BlockSpec((1, positions, row_width), row5),
            ]
            + [ANY] * (replicas + 1),
            out_specs=pl.BlockSpec((1, positions, queries.shape[2]), row5),
            scratch_shapes=[
                pltpu.VMEM((2, 2, most * page_len, row_width), bf16),
                pltpu.SemaphoreType.DMA((2,)),
            ],
        ),
        cost_estimate=pl.CostEstimate(
            flops=4 * count * positions * queries.shape[2] * (most * page_len + positions),
            bytes_accessed=count * (positions * queries.shape[2] * 4 + most * page_len * row_width * 4),
            transcendentals=count * positions * kv_here * per_kv * (most * page_len + positions),
        ),
        compiler_params=PARAMS,
        name="attention",
    )(
        plan,
        prefix_pages,
        suffix_length,
        page_rows,
        queries,
        suffix_keys,
        suffix_values,
        *[pages[s] for s in steps],
        page_keys,
        page_values,
    )

    mamba_output = None
    for members in (list(range(half)), list(range(half, replicas))):
        chained = 0 if mamba_output is None else 1
        mamba_output = pl.pallas_call(
            functools.partial(finish_kernel, replicas, slots, members, chained),
            out_shape=shape((count, positions, channels), bf16),
            in_specs=[SMEM] * 2 + [VMEM] * (3 + len(members)) + [ANY] * chained,
            out_specs=ANY,
            scratch_shapes=[pltpu.VMEM((count, positions, channels), bf16), pltpu.SemaphoreType.DMA],
            input_output_aliases={5 + len(members): 0} if chained else {},
            compiler_params=PARAMS,
            cost_estimate=pl.CostEstimate(
                flops=len(members) * slots * positions * channels * 8,
                bytes_accessed=len(members) * slots * positions * channels * 12,
                transcendentals=0,
            ),
            name="finish",
        )(
            plan,
            suffix_length,
            norm_gain.reshape(1, channels),
            fixed,
            scaled,
            *[carried[s] for s in members],
            *([mamba_output] if chained else []),
        )
    return (mamba_output, attention_output)


def solution(mesh):
    return jax.shard_map(
        per_device,
        mesh=mesh,
        in_specs=(
            P("groups", None),
            P("groups"),
            P(("groups", "replica")),
            P("groups", None),
            P(("groups", "replica")),
            P(("groups", "replica"), "tensor", None, None),
            P(("groups", "replica"), None, "tensor"),
            P(("groups", "replica"), None, "tensor"),
            P(("groups", "replica"), None, "tensor"),
            P(("groups", "replica"), None, "tensor"),
            P("tensor"),
            P(("groups", "replica"), None, "tensor"),
            P(("groups", "replica"), None, "tensor"),
            P("tensor"),
            P(("groups", "replica"), None, "tensor"),
            P("tensor"),
            P(("groups", "replica"), None, "tensor"),
            P(("groups", "replica"), None, "tensor"),
            P(("groups", "replica"), None, "tensor"),
        ),
        out_specs=(
            P(("groups", "replica"), None, "tensor"),
            P(("groups", "replica"), None, "tensor"),
        ),
        check_vma=False,
    )
```

```python
import functools
import math

import jax
import jax.numpy as jnp
from jax import lax
from jax.experimental import pallas as pl
from jax.experimental.pallas import tpu as pltpu
from jax.sharding import PartitionSpec as P

STATE = 128
HEAD_DIM = 128
MIB = 1 << 20

ANY = pl.BlockSpec(memory_space=pl.ANY)
VMEM = pl.BlockSpec(memory_space=pltpu.VMEM)
SMEM = pl.BlockSpec(memory_space=pltpu.SMEM)
WIDE = pltpu.CompilerParams(vmem_limit_bytes=60 * MIB)
PARAMS = pltpu.CompilerParams(vmem_limit_bytes=24 * MIB)


def partner_steps(replicas):
    return [s ^ 1 if s > 1 else s for s in range(replicas - 1, 0, -1)]


def places(replicas, slots, count):
    state = 0
    source = state + replicas * slots
    rank = source + count
    order = rank + count
    ends = order + count
    return state, source, rank, order, ends, ends + replicas


def pack_pages(replicas, slots, count, most, page_len, steps, me, holder_ref, pages_ref, pools, packed, outs, sems):
    keys, values = pools
    copies = []
    for at, step in enumerate(steps):
        first = lax.bitwise_xor(me, step) * count

        def serve(j, rank_here, at=at, first=first):
            request = first + j
            hit = holder_ref[0, request] == me

            @pl.when(hit)
            def _():
                slot = jnp.minimum(rank_here, slots - 1)
                for place in range(most):
                    page = pages_ref[place, request]
                    rows = slice(place * page_len, (place + 1) * page_len)
                    packed[at, slot, 0, rows, :] = keys[page]
                    packed[at, slot, 1, rows, :] = values[page]

            return rank_here + hit.astype(jnp.int32)

        lax.fori_loop(0, count, serve, jnp.int32(0))
        copies.append(pltpu.make_async_copy(packed.at[at], outs[at], sems.at[at]))
        copies[-1].start()
    return copies


def clear(ref, length):
    def body(i, carry):
        ref[i] = 0
        return carry

    lax.fori_loop(0, length, body, 0)


def first_kernel(
    replicas,
    slots,
    count,
    most,
    page_len,
    far,
    me_ref,
    holder_ref,
    pages_ref,
    keys_hbm,
    values_hbm,
    reads_hbm,
    *rest,
):
    steps = partner_steps(replicas)
    page_out, rest = rest[: len(far)], rest[len(far) :]
    read_out, rest = dict(zip(steps, rest[: replicas - 1])), rest[replicas - 1 :]
    keys, values, packed, seen, reads, sems, page_sems = rest
    loads = [
        pltpu.make_async_copy(keys_hbm, keys, sems.at[0]),
        pltpu.make_async_copy(values_hbm, values, sems.at[1]),
        pltpu.make_async_copy(reads_hbm, reads, sems.at[2]),
    ]
    for load in loads:
        load.start()
    me = me_ref[0]
    clear(seen, replicas)
    for load in loads:
        load.wait()
    copies = pack_pages(
        replicas, slots, count, most, page_len, far, me, holder_ref, pages_ref, (keys, values), packed, page_out, page_sems
    )

    def ask(j, sent):
        step = lax.bitwise_xor(me, holder_ref[0, me * count + j])
        slot = jnp.minimum(seen[step], slots - 1)
        seen[step] = slot + 1
        for known in steps:

            @pl.when(step == known)
            def _(known=known):
                pltpu.make_async_copy(reads.at[j], read_out[known].at[slot], sems.at[3]).start()

        return sent + (step != 0).astype(jnp.int32)

    sent = lax.fori_loop(0, count, ask, jnp.int32(0))

    def wait_read(i, carry):
        pltpu.make_async_copy(reads.at[0], read_out[steps[0]].at[0], sems.at[3]).wait()
        return carry

    lax.fori_loop(0, sent, wait_read, 0)
    for copy in copies:
        copy.wait()


def second_kernel(
    replicas,
    slots,
    count,
    most,
    page_len,
    near,
    waited,
    me_ref,
    holder_ref,
    slot_ref,
    pages_ref,
    keys_hbm,
    values_hbm,
    *rest,
):
    page_out = rest[waited : waited + len(near)]
    plan, keys, values, packed, seen, sems, page_sems = rest[waited + len(near) :]
    state, source, rank, order, ends, mine = places(replicas, slots, count)
    loads = [
        pltpu.make_async_copy(keys_hbm, keys, sems.at[0]),
        pltpu.make_async_copy(values_hbm, values, sems.at[1]),
    ]
    for load in loads:
        load.start()
    me = me_ref[0]
    plan[mine] = me
    clear(plan, replicas * slots)
    clear(seen, replicas)
    for load in loads:
        load.wait()
    copies = pack_pages(
        replicas, slots, count, most, page_len, near, me, holder_ref, pages_ref, (keys, values), packed, page_out, page_sems
    )
    for step in range(replicas):
        first = lax.bitwise_xor(me, step) * count

        def serve(j, rank_here, step=step, first=first):
            hit = holder_ref[0, first + j] == me

            @pl.when(hit)
            def _():
                plan[state + step * slots + jnp.minimum(rank_here, slots - 1)] = slot_ref[first + j]

            return rank_here + hit.astype(jnp.int32)

        lax.fori_loop(0, count, serve, jnp.int32(0))

    def ask(j, carry):
        step = lax.bitwise_xor(me, holder_ref[0, me * count + j])
        slot = jnp.minimum(seen[step], slots - 1)
        seen[step] = slot + 1
        plan[source + j] = step
        plan[rank + j] = slot
        return carry

    lax.fori_loop(0, count, ask, 0)
    place = jnp.int32(0)
    for step in range(replicas):

        def put(j, at, step=step):
            hit = plan[source + j] == step

            @pl.when(hit)
            def _():
                plan[order + at] = j

            return at + hit.astype(jnp.int32)

        place = lax.fori_loop(0, count, put, place)
        plan[ends + step] = place
    for copy in copies:
        copy.wait()


def carried_kernel(replicas, slots, count, steps, plan_ref, *rest):
    at_state, _, _, at_order, _, _ = places(replicas, slots, count)
    reads_hbm, states_hbm = rest[: len(steps)], rest[len(steps)]
    outs = rest[-3 - len(steps) : -3]
    reads, states, sems = rest[-3:]
    channels = states.shape[1]
    positions = reads.shape[2]
    copies = []
    for n, step in enumerate(steps):
        copies.append([])
        for k in range(slots):
            which = k if step else plan_ref[at_order + k]
            state = plan_ref[at_state + step * slots + k]
            copies[n].append(pltpu.make_async_copy(reads_hbm[n].at[which], reads.at[n, k], sems.at[n, 2 * k]))
            copies[n].append(
                pltpu.make_async_copy(
                    states_hbm.at[state],
                    states.at[n, :, k * STATE : (k + 1) * STATE],
                    sems.at[n, 2 * k + 1],
                )
            )
        for copy in copies[n]:
            copy.start()
    blank = jnp.zeros((positions, STATE), jnp.bfloat16)
    spare = STATE - slots * positions
    tile = 512
    for n in range(len(steps)):
        for copy in copies[n]:
            copy.wait()
        rows = [
            jnp.concatenate([reads[n, k] if j == k else blank for j in range(slots)], axis=1)
            for k in range(slots)
        ]
        if spare:
            rows.append(jnp.zeros((spare, slots * STATE), jnp.bfloat16))
        maps = jnp.concatenate(rows, axis=0)
        for first in range(0, channels, tile):
            product = lax.dot_general(
                states[n, first : first + tile],
                maps,
                (((1,), (1,)), ((), ())),
                preferred_element_type=jnp.float32,
            ).T.astype(jnp.bfloat16)
            for k in range(slots):
                outs[n][k, :, first : first + tile] = product[k * positions : (k + 1) * positions]


def attention_kernel(
    replicas,
    kv_here,
    per_kv,
    page_len,
    most,
    slots,
    plan_ref,
    count_ref,
    live_ref,
    pages_ref,
    query_ref,
    key_ref,
    value_ref,
    *rest,
):
    steps = partner_steps(replicas)
    arrived = dict(zip(steps, rest[: replicas - 1]))
    pool_keys, pool_values, out_ref, buffer, sems = rest[replicas - 1 :]
    i, total = pl.program_id(0), pl.num_programs(0)
    _, at_source, at_rank, _, _, at_me = places(replicas, slots, count_ref.shape[0])

    def fetch(j, slot):
        step, rank = plan_ref[at_source + j], plan_ref[at_rank + j]
        request = plan_ref[at_me] * count_ref.shape[0] + j
        for known in steps:

            @pl.when(step == known)
            def _(known=known):
                pltpu.make_async_copy(arrived[known].at[rank], buffer.at[slot], sems.at[slot]).start()

        @pl.when(step == 0)
        def _():
            for place in range(most):
                page = pages_ref[place, request]
                rows = pl.ds(place * page_len, page_len)
                pltpu.make_async_copy(pool_keys.at[page], buffer.at[slot, 0, rows], sems.at[slot]).start()
                pltpu.make_async_copy(pool_values.at[page], buffer.at[slot, 1, rows], sems.at[slot]).start()

    @pl.when(i == 0)
    def _():
        fetch(i, 0)

    @pl.when(i + 1 < total)
    def _():
        fetch(i + 1, lax.rem(i + 1, 2))

    now = lax.rem(i, 2)
    pltpu.make_async_copy(buffer.at[now], buffer.at[now], sems.at[now]).wait()

    positions = query_ref.shape[1]
    rows = per_kv * positions
    cached = most * page_len
    live = live_ref[i]
    scale = math.log2(math.e) / math.sqrt(HEAD_DIM)
    column = lax.broadcasted_iota(jnp.int32, (rows, cached), 1)
    ahead = column < count_ref[i] * page_len
    row = lax.broadcasted_iota(jnp.int32, (rows, positions), 0) & (positions - 1)
    causal = lax.broadcasted_iota(jnp.int32, (rows, positions), 1) <= row
    alive = (lax.broadcasted_iota(jnp.int32, (rows, HEAD_DIM), 0) & (positions - 1)) < live
    contract = (((1,), (1,)), ((), ()))
    for g in range(kv_here):
        lanes = slice(g * HEAD_DIM, (g + 1) * HEAD_DIM)
        heads = [(g * per_kv + q) * HEAD_DIM for q in range(per_kv)]
        query = jnp.concatenate([query_ref[0, :, h : h + HEAD_DIM] for h in heads], axis=0)
        old_keys, old_values = buffer[now, 0, :, lanes], buffer[now, 1, :, lanes]
        new_keys, new_values = key_ref[0, :, lanes], value_ref[0, :, lanes]
        old = lax.dot_general(query, old_keys, contract, preferred_element_type=jnp.float32)
        new = lax.dot_general(query, new_keys, contract, preferred_element_type=jnp.float32)
        old = jnp.where(ahead, old, -1e30)
        new = jnp.where(causal, new, -1e30)
        top = jnp.maximum(jnp.max(old, axis=1, keepdims=True), jnp.max(new, axis=1, keepdims=True))
        old, new = jnp.exp2((old - top) * scale), jnp.exp2((new - top) * scale)
        share = 1.0 / (jnp.sum(old, axis=1, keepdims=True) + jnp.sum(new, axis=1, keepdims=True))
        old, new = (old * share).astype(jnp.bfloat16), (new * share).astype(jnp.bfloat16)
        result = jnp.dot(old, old_values, preferred_element_type=jnp.float32) + jnp.dot(
            new, new_values, preferred_element_type=jnp.float32
        )
        result = jnp.where(alive, result, 0.0).astype(out_ref.dtype)
        for q, h in enumerate(heads):
            out_ref[0, :, h : h + HEAD_DIM] = result[q * positions : (q + 1) * positions]


def halves(x):
    high = x.astype(jnp.bfloat16)
    return high, (x - high.astype(jnp.float32)).astype(jnp.bfloat16)


def within_kernel(
    rate_ref, skip_ref, spread_ref, step_ref, read_ref, write_ref, input_ref, gate_ref, fixed_ref, scaled_ref
):
    positions = input_ref.shape[1]
    heads = step_ref.shape[2]
    step = step_ref[0]
    later = lax.broadcasted_iota(jnp.int32, (positions, positions), 0)
    earlier = lax.broadcasted_iota(jnp.int32, (positions, positions), 1)
    causal = earlier <= later
    decays = step * (-jnp.exp(rate_ref[...]))
    running = lax.dot_general(
        causal.astype(jnp.float32),
        decays,
        (((1,), (0,)), ((), ())),
        precision=lax.Precision.HIGHEST,
        preferred_element_type=jnp.float32,
    )
    decay = jnp.exp(running)
    growth = jnp.exp(-running) * step
    both = jnp.concatenate([decay, growth], axis=0)
    high, low = halves(both)
    wide = jnp.dot(
        jnp.concatenate([high, low], axis=1), spread_ref[...], preferred_element_type=jnp.float32
    )
    decay, growth = wide[:positions], wide[positions:]
    contact = lax.dot_general(
        read_ref[0], write_ref[0], (((1,), (1,)), ((), ())), preferred_element_type=jnp.float32
    )
    contact = jnp.where(causal, contact, 0.0)
    contact_high, contact_low = halves(contact)
    inputs = input_ref[0].astype(jnp.float32)
    weighed = (inputs * growth).astype(jnp.bfloat16)
    within = jnp.dot(
        jnp.concatenate([contact_high, contact_low], axis=1),
        jnp.concatenate([weighed, weighed], axis=0),
        preferred_element_type=jnp.float32,
    )
    gate = gate_ref[0].astype(jnp.float32)
    gate = gate / (1.0 + jnp.exp(-gate))
    fixed_ref[0] = gate * (decay * within + skip_ref[...] * inputs)
    scaled_ref[0] = gate * decay


def finish_kernel(
    replicas, slots, members, chained, plan_ref, live_ref, gain_ref, fixed_ref, scaled_ref, *rest
):
    count = live_ref.shape[0]
    _, at_source, at_rank, at_order, at_ends, _ = places(replicas, slots, count)
    arrived = dict(zip(members, rest[: len(members)]))
    out_ref, ready, sem = rest[len(members) + chained :]
    positions, channels = fixed_ref.shape[1:]
    first = plan_ref[at_ends + members[0] - 1] if members[0] else 0
    last = plan_ref[at_ends + members[-1]]

    def copy(i):
        request = plan_ref[at_order + i]
        return pltpu.make_async_copy(ready.at[request], out_ref.at[request], sem)

    def finish(i, carry):
        request = plan_ref[at_order + i]
        alive = lax.broadcasted_iota(jnp.int32, (positions, 1), 0) < live_ref[request]
        for known in members:

            @pl.when(plan_ref[at_source + request] == known)
            def _(known=known):
                carried = arrived[known][plan_ref[at_rank + request]].astype(jnp.float32)
                gated = fixed_ref[request] + scaled_ref[request] * carried
                square = jnp.sum(gated * gated, axis=1, keepdims=True) * (1.0 / channels)
                factor = jnp.where(alive, lax.rsqrt(square + 1e-05), 0.0)
                ready[request] = (gated * factor * gain_ref[...]).astype(out_ref.dtype)

        copy(i).start()
        return carry

    lax.fori_loop(first, last, finish, 0)

    def wait(i, carry):
        copy(i).wait()
        return carry

    lax.fori_loop(first, last, wait, 0)


def per_device(
    holder,
    cache_slot,
    prefix_pages,
    page_ids,
    suffix_length,
    cache_states,
    page_keys,
    page_values,
    ssm_inputs,
    step_sizes,
    log_rates,
    write_map,
    read_map,
    skip_gain,
    gate_values,
    norm_gain,
    queries,
    suffix_keys,
    suffix_values,
):
    replicas = lax.axis_size("replica")
    assert replicas & (replicas - 1) == 0
    myself = lax.axis_index("replica").astype(jnp.int32)
    count, positions, channels = ssm_inputs.shape
    slots = (count + replicas - 1) // replicas
    heads = log_rates.shape[0]
    width = channels // heads
    assert write_map.shape[2] == STATE
    page_len, row_width = page_keys.shape[1:]
    most = page_ids.shape[1]
    kv_here = row_width // HEAD_DIM
    per_kv = queries.shape[2] // row_width
    bf16, f32 = jnp.bfloat16, jnp.float32
    steps = partner_steps(replicas)
    shape = jax.ShapeDtypeStruct

    me = myself.reshape(1)
    holder_row = holder.T
    page_rows = page_ids.T
    def exchange(x, step):
        return lax.ppermute(x, "replica", [(i, i ^ step) for i in range(replicas)])

    at_state, at_source, at_rank, at_order, at_ends, at_me = places(replicas, slots, count)
    third = max(1, (replicas - 1) // 3)
    far, near = steps[:third], steps[third:]
    page_shape = shape((slots, 2, most * page_len, row_width), bf16)
    first = pl.pallas_call(
        functools.partial(first_kernel, replicas, slots, count, most, page_len, far),
        out_shape=[page_shape] * len(far) + [shape((slots, positions, STATE), bf16)] * (replicas - 1),
        in_specs=[SMEM] * 3 + [ANY] * 3,
        out_specs=[ANY] * (len(far) + replicas - 1),
        scratch_shapes=[
            pltpu.VMEM(page_keys.shape, bf16),
            pltpu.VMEM(page_values.shape, bf16),
            pltpu.VMEM((len(far), *page_shape.shape), bf16),
            pltpu.SMEM((replicas,), jnp.int32),
            pltpu.VMEM(read_map.shape, bf16),
            pltpu.SemaphoreType.DMA((4,)),
            pltpu.SemaphoreType.DMA((len(far),)),
        ],
        compiler_params=WIDE,
        name="first",
    )(me, holder_row, page_rows, page_keys, page_values, read_map)
    pages = {s: exchange(x, s) for s, x in zip(far, first)}
    reads = {s: exchange(x, s) for s, x in zip(steps, first[len(far) :])}
    waited = []
    second = pl.pallas_call(
        functools.partial(second_kernel, replicas, slots, count, most, page_len, near, len(waited)),
        out_shape=[page_shape] * len(near) + [shape((at_me + 1,), jnp.int32)],
        in_specs=[SMEM] * 4 + [ANY] * (2 + len(waited)),
        out_specs=[ANY] * len(near) + [SMEM],
        scratch_shapes=[
            pltpu.VMEM(page_keys.shape, bf16),
            pltpu.VMEM(page_values.shape, bf16),
            pltpu.VMEM((len(near), *page_shape.shape), bf16),
            pltpu.SMEM((replicas,), jnp.int32),
            pltpu.SemaphoreType.DMA((2,)),
            pltpu.SemaphoreType.DMA((len(near),)),
        ],
        compiler_params=WIDE,
        name="second",
    )(me, holder_row, cache_slot, page_rows, page_keys, page_values, *waited)
    pages.update({s: exchange(x, s) for s, x in zip(near, second[:-1])})
    reads[0] = read_map
    plan = second[-1]

    states = cache_states.reshape(cache_states.shape[0], channels, STATE)
    carried = {}
    token = []
    half = max(1, replicas // 2)
    for served in (steps + [0],):
        results = pl.pallas_call(
            functools.partial(carried_kernel, replicas, slots, count, served),
            out_shape=[shape((slots, positions, channels), bf16)] * len(served),
            grid_spec=pltpu.PrefetchScalarGridSpec(
                num_scalar_prefetch=1,
                grid=(1,),
                in_specs=[ANY] * (len(served) + 1 + len(token)),
                out_specs=[pl.BlockSpec((slots, positions, channels), lambda i, plan: (0, 0, 0))] * len(served),
                scratch_shapes=[
                    pltpu.VMEM((len(served), slots, positions, STATE), bf16),
                    pltpu.VMEM((len(served), channels, slots * STATE), bf16),
                    pltpu.SemaphoreType.DMA((len(served), 2 * slots)),
                ],
            ),
            compiler_params=WIDE,
            cost_estimate=pl.CostEstimate(
                flops=64 * len(served) * slots * positions * channels * STATE,
                bytes_accessed=2 * len(served) * slots * channels * (STATE + positions),
                transcendentals=0,
            ),
            name="carried",
        )(plan, *[reads[s] for s in served], states, *token)
        token = [results[0]]
        for s, x in zip(served, results):
            carried[s] = exchange(x, s) if s else x

    spread = (jnp.arange(2 * heads)[:, None] % heads == jnp.arange(channels)[None, :] // width).astype(bf16)
    skip_wide = jnp.repeat(skip_gain, width).reshape(1, channels)
    row = lambda i: (i, 0, 0)
    whole = lambda i: (0, 0)
    fixed, scaled = pl.pallas_call(
        within_kernel,
        out_shape=[shape((count, positions, channels), f32)] * 2,
        grid=(count,),
        in_specs=[
            pl.BlockSpec((1, heads), whole),
            pl.BlockSpec((1, channels), whole),
            pl.BlockSpec((2 * heads, channels), whole),
            pl.BlockSpec((1, positions, heads), row),
            pl.BlockSpec((1, positions, STATE), row),
            pl.BlockSpec((1, positions, STATE), row),
            pl.BlockSpec((1, positions, channels), row),
            pl.BlockSpec((1, positions, channels), row),
        ],
        out_specs=[pl.BlockSpec((1, positions, channels), row)] * 2,
        cost_estimate=pl.CostEstimate(
            flops=2 * count * positions * channels * positions * 8,
            bytes_accessed=count * positions * channels * 12,
            transcendentals=count * positions * channels,
        ),
        compiler_params=PARAMS,
        name="within",
    )(
        log_rates.reshape(1, heads),
        skip_wide,
        spread,
        step_sizes,
        read_map,
        write_map,
        ssm_inputs,
        gate_values,
    )

    row5 = lambda i, *refs: (i, 0, 0)
    attention_output = pl.pallas_call(
        functools.partial(attention_kernel, replicas, kv_here, per_kv, page_len, most, slots),
        out_shape=shape((count, positions, queries.shape[2]), bf16),
        grid_spec=pltpu.PrefetchScalarGridSpec(
            num_scalar_prefetch=4,
            grid=(count,),
            in_specs=[
                pl.BlockSpec((1, positions, queries.shape[2]), row5),
                pl.BlockSpec((1, positions, row_width), row5),
                pl.BlockSpec((1, positions, row_width), row5),
            ]
            + [ANY] * (replicas + 1),
            out_specs=pl.BlockSpec((1, positions, queries.shape[2]), row5),
            scratch_shapes=[
                pltpu.VMEM((2, 2, most * page_len, row_width), bf16),
                pltpu.SemaphoreType.DMA((2,)),
            ],
        ),
        cost_estimate=pl.CostEstimate(
            flops=4 * count * positions * queries.shape[2] * (most * page_len + positions),
            bytes_accessed=count * (positions * queries.shape[2] * 4 + most * page_len * row_width * 4),
            transcendentals=count * positions * kv_here * per_kv * (most * page_len + positions),
        ),
        compiler_params=PARAMS,
        name="attention",
    )(
        plan,
        prefix_pages,
        suffix_length,
        page_rows,
        queries,
        suffix_keys,
        suffix_values,
        *[pages[s] for s in steps],
        page_keys,
        page_values,
    )

    mamba_output = None
    for members in (list(range(half)), list(range(half, replicas))):
        chained = 0 if mamba_output is None else 1
        mamba_output = pl.pallas_call(
            functools.partial(finish_kernel, replicas, slots, members, chained),
            out_shape=shape((count, positions, channels), bf16),
            in_specs=[SMEM] * 2 + [VMEM] * (3 + len(members)) + [ANY] * chained,
            out_specs=ANY,
            scratch_shapes=[pltpu.VMEM((count, positions, channels), bf16), pltpu.SemaphoreType.DMA],
            input_output_aliases={5 + len(members): 0} if chained else {},
            compiler_params=PARAMS,
            cost_estimate=pl.CostEstimate(
                flops=len(members) * slots * positions * channels * 8,
                bytes_accessed=len(members) * slots * positions * channels * 12,
                transcendentals=0,
            ),
            name="finish",
        )(
            plan,
            suffix_length,
            norm_gain.reshape(1, channels),
            fixed,
            scaled,
            *[carried[s] for s in members],
            *([mamba_output] if chained else []),
        )
    return (mamba_output, attention_output)


def solution(mesh):
    return jax.shard_map(
        per_device,
        mesh=mesh,
        in_specs=(
            P("groups", None),
            P("groups"),
            P(("groups", "replica")),
            P("groups", None),
            P(("groups", "replica")),
            P(("groups", "replica"), "tensor", None, None),
            P(("groups", "replica"), None, "tensor"),
            P(("groups", "replica"), None, "tensor"),
            P(("groups", "replica"), None, "tensor"),
            P(("groups", "replica"), None, "tensor"),
            P("tensor"),
            P(("groups", "replica"), None, "tensor"),
            P(("groups", "replica"), None, "tensor"),
            P("tensor"),
            P(("groups", "replica"), None, "tensor"),
            P("tensor"),
            P(("groups", "replica"), None, "tensor"),
            P(("groups", "replica"), None, "tensor"),
            P(("groups", "replica"), None, "tensor"),
        ),
        out_specs=(
            P(("groups", "replica"), None, "tensor"),
            P(("groups", "replica"), None, "tensor"),
        ),
        check_vma=False,
    )
```

```python
import functools
import math

import jax
import jax.numpy as jnp
from jax import lax
from jax.experimental import pallas as pl
from jax.experimental.pallas import tpu as pltpu
from jax.sharding import PartitionSpec as P

STATE = 128
HEAD_DIM = 128
MIB = 1 << 20

ANY = pl.BlockSpec(memory_space=pl.ANY)
VMEM = pl.BlockSpec(memory_space=pltpu.VMEM)
SMEM = pl.BlockSpec(memory_space=pltpu.SMEM)
WIDE = pltpu.CompilerParams(vmem_limit_bytes=60 * MIB)
PARAMS = pltpu.CompilerParams(vmem_limit_bytes=24 * MIB)


def partner_steps(replicas):
    return list(range(replicas - 1, 0, -1))


def places(replicas, slots, count):
    state = 0
    source = state + replicas * slots
    rank = source + count
    order = rank + count
    ends = order + count
    return state, source, rank, order, ends, ends + replicas


def pack_pages(replicas, slots, count, most, page_len, steps, me, holder_ref, pages_ref, pools, packed, outs, sems):
    keys, values = pools
    copies = []
    for at, step in enumerate(steps):
        first = lax.bitwise_xor(me, step) * count

        def serve(j, rank_here, at=at, first=first):
            request = first + j
            hit = holder_ref[0, request] == me

            @pl.when(hit)
            def _():
                slot = jnp.minimum(rank_here, slots - 1)
                for place in range(most):
                    page = pages_ref[place, request]
                    rows = slice(place * page_len, (place + 1) * page_len)
                    packed[at, slot, 0, rows, :] = keys[page]
                    packed[at, slot, 1, rows, :] = values[page]

            return rank_here + hit.astype(jnp.int32)

        lax.fori_loop(0, count, serve, jnp.int32(0))
        copies.append(pltpu.make_async_copy(packed.at[at], outs[at], sems.at[at]))
        copies[-1].start()
    return copies


def clear(ref, length):
    def body(i, carry):
        ref[i] = 0
        return carry

    lax.fori_loop(0, length, body, 0)


def first_kernel(
    replicas,
    slots,
    count,
    most,
    page_len,
    far,
    me_ref,
    holder_ref,
    pages_ref,
    keys_hbm,
    values_hbm,
    reads_hbm,
    *rest,
):
    steps = partner_steps(replicas)
    page_out, rest = rest[: len(far)], rest[len(far) :]
    read_out, rest = dict(zip(steps, rest[: replicas - 1])), rest[replicas - 1 :]
    keys, values, packed, seen, reads, sems, page_sems = rest
    loads = [
        pltpu.make_async_copy(keys_hbm, keys, sems.at[0]),
        pltpu.make_async_copy(values_hbm, values, sems.at[1]),
        pltpu.make_async_copy(reads_hbm, reads, sems.at[2]),
    ]
    for load in loads:
        load.start()
    me = me_ref[0]
    clear(seen, replicas)
    for load in loads:
        load.wait()
    copies = pack_pages(
        replicas, slots, count, most, page_len, far, me, holder_ref, pages_ref, (keys, values), packed, page_out, page_sems
    )

    def ask(j, sent):
        step = lax.bitwise_xor(me, holder_ref[0, me * count + j])
        slot = jnp.minimum(seen[step], slots - 1)
        seen[step] = slot + 1
        for known in steps:

            @pl.when(step == known)
            def _(known=known):
                pltpu.make_async_copy(reads.at[j], read_out[known].at[slot], sems.at[3]).start()

        return sent + (step != 0).astype(jnp.int32)

    sent = lax.fori_loop(0, count, ask, jnp.int32(0))

    def wait_read(i, carry):
        pltpu.make_async_copy(reads.at[0], read_out[steps[0]].at[0], sems.at[3]).wait()
        return carry

    lax.fori_loop(0, sent, wait_read, 0)
    for copy in copies:
        copy.wait()


def second_kernel(
    replicas,
    slots,
    count,
    most,
    page_len,
    near,
    waited,
    me_ref,
    holder_ref,
    slot_ref,
    pages_ref,
    keys_hbm,
    values_hbm,
    *rest,
):
    page_out = rest[waited : waited + len(near)]
    plan, keys, values, packed, seen, sems, page_sems = rest[waited + len(near) :]
    state, source, rank, order, ends, mine = places(replicas, slots, count)
    loads = [
        pltpu.make_async_copy(keys_hbm, keys, sems.at[0]),
        pltpu.make_async_copy(values_hbm, values, sems.at[1]),
    ]
    for load in loads:
        load.start()
    me = me_ref[0]
    plan[mine] = me
    clear(plan, replicas * slots)
    clear(seen, replicas)
    for load in loads:
        load.wait()
    copies = pack_pages(
        replicas, slots, count, most, page_len, near, me, holder_ref, pages_ref, (keys, values), packed, page_out, page_sems
    )
    for step in range(replicas):
        first = lax.bitwise_xor(me, step) * count

        def serve(j, rank_here, step=step, first=first):
            hit = holder_ref[0, first + j] == me

            @pl.when(hit)
            def _():
                plan[state + step * slots + jnp.minimum(rank_here, slots - 1)] = slot_ref[first + j]

            return rank_here + hit.astype(jnp.int32)

        lax.fori_loop(0, count, serve, jnp.int32(0))

    def ask(j, carry):
        step = lax.bitwise_xor(me, holder_ref[0, me * count + j])
        slot = jnp.minimum(seen[step], slots - 1)
        seen[step] = slot + 1
        plan[source + j] = step
        plan[rank + j] = slot
        return carry

    lax.fori_loop(0, count, ask, 0)
    place = jnp.int32(0)
    for step in range(replicas):

        def put(j, at, step=step):
            hit = plan[source + j] == step

            @pl.when(hit)
            def _():
                plan[order + at] = j

            return at + hit.astype(jnp.int32)

        place = lax.fori_loop(0, count, put, place)
        plan[ends + step] = place
    for copy in copies:
        copy.wait()


def carried_kernel(replicas, slots, count, steps, plan_ref, *rest):
    at_state, _, _, at_order, _, _ = places(replicas, slots, count)
    reads_hbm, states_hbm = rest[: len(steps)], rest[len(steps)]
    outs = rest[-3 - len(steps) : -3]
    reads, states, sems = rest[-3:]
    channels = states.shape[1]
    positions = reads.shape[2]
    copies = []
    for n, step in enumerate(steps):
        copies.append([])
        for k in range(slots):
            which = k if step else plan_ref[at_order + k]
            state = plan_ref[at_state + step * slots + k]
            copies[n].append(pltpu.make_async_copy(reads_hbm[n].at[which], reads.at[n, k], sems.at[n, 2 * k]))
            copies[n].append(
                pltpu.make_async_copy(
                    states_hbm.at[state],
                    states.at[n, :, k * STATE : (k + 1) * STATE],
                    sems.at[n, 2 * k + 1],
                )
            )
        for copy in copies[n]:
            copy.start()
    blank = jnp.zeros((positions, STATE), jnp.bfloat16)
    spare = STATE - slots * positions
    tile = 512
    for n in range(len(steps)):
        for copy in copies[n]:
            copy.wait()
        rows = [
            jnp.concatenate([reads[n, k] if j == k else blank for j in range(slots)], axis=1)
            for k in range(slots)
        ]
        if spare:
            rows.append(jnp.zeros((spare, slots * STATE), jnp.bfloat16))
        maps = jnp.concatenate(rows, axis=0)
        for first in range(0, channels, tile):
            product = lax.dot_general(
                states[n, first : first + tile],
                maps,
                (((1,), (1,)), ((), ())),
                preferred_element_type=jnp.float32,
            ).T.astype(jnp.bfloat16)
            for k in range(slots):
                outs[n][k, :, first : first + tile] = product[k * positions : (k + 1) * positions]


def attention_kernel(
    replicas,
    kv_here,
    per_kv,
    page_len,
    most,
    slots,
    plan_ref,
    count_ref,
    live_ref,
    pages_ref,
    query_ref,
    key_ref,
    value_ref,
    *rest,
):
    steps = partner_steps(replicas)
    arrived = dict(zip(steps, rest[: replicas - 1]))
    pool_keys, pool_values, out_ref, buffer, sems = rest[replicas - 1 :]
    i, total = pl.program_id(0), pl.num_programs(0)
    _, at_source, at_rank, _, _, at_me = places(replicas, slots, count_ref.shape[0])

    def fetch(j, slot):
        step, rank = plan_ref[at_source + j], plan_ref[at_rank + j]
        request = plan_ref[at_me] * count_ref.shape[0] + j
        for known in steps:

            @pl.when(step == known)
            def _(known=known):
                pltpu.make_async_copy(arrived[known].at[rank], buffer.at[slot], sems.at[slot]).start()

        @pl.when(step == 0)
        def _():
            for place in range(most):
                page = pages_ref[place, request]
                rows = pl.ds(place * page_len, page_len)
                pltpu.make_async_copy(pool_keys.at[page], buffer.at[slot, 0, rows], sems.at[slot]).start()
                pltpu.make_async_copy(pool_values.at[page], buffer.at[slot, 1, rows], sems.at[slot]).start()

    @pl.when(i == 0)
    def _():
        fetch(i, 0)

    @pl.when(i + 1 < total)
    def _():
        fetch(i + 1, lax.rem(i + 1, 2))

    now = lax.rem(i, 2)
    pltpu.make_async_copy(buffer.at[now], buffer.at[now], sems.at[now]).wait()

    positions = query_ref.shape[1]
    rows = per_kv * positions
    cached = most * page_len
    live = live_ref[i]
    scale = math.log2(math.e) / math.sqrt(HEAD_DIM)
    column = lax.broadcasted_iota(jnp.int32, (rows, cached), 1)
    ahead = column < count_ref[i] * page_len
    row = lax.broadcasted_iota(jnp.int32, (rows, positions), 0) & (positions - 1)
    causal = lax.broadcasted_iota(jnp.int32, (rows, positions), 1) <= row
    alive = (lax.broadcasted_iota(jnp.int32, (rows, HEAD_DIM), 0) & (positions - 1)) < live
    contract = (((1,), (1,)), ((), ()))
    for g in range(kv_here):
        lanes = slice(g * HEAD_DIM, (g + 1) * HEAD_DIM)
        heads = [(g * per_kv + q) * HEAD_DIM for q in range(per_kv)]
        query = jnp.concatenate([query_ref[0, :, h : h + HEAD_DIM] for h in heads], axis=0)
        old_keys, old_values = buffer[now, 0, :, lanes], buffer[now, 1, :, lanes]
        new_keys, new_values = key_ref[0, :, lanes], value_ref[0, :, lanes]
        old = lax.dot_general(query, old_keys, contract, preferred_element_type=jnp.float32)
        new = lax.dot_general(query, new_keys, contract, preferred_element_type=jnp.float32)
        old = jnp.where(ahead, old, -1e30)
        new = jnp.where(causal, new, -1e30)
        top = jnp.maximum(jnp.max(old, axis=1, keepdims=True), jnp.max(new, axis=1, keepdims=True))
        old, new = jnp.exp2((old - top) * scale), jnp.exp2((new - top) * scale)
        share = 1.0 / (jnp.sum(old, axis=1, keepdims=True) + jnp.sum(new, axis=1, keepdims=True))
        old, new = (old * share).astype(jnp.bfloat16), (new * share).astype(jnp.bfloat16)
        result = jnp.dot(old, old_values, preferred_element_type=jnp.float32) + jnp.dot(
            new, new_values, preferred_element_type=jnp.float32
        )
        result = jnp.where(alive, result, 0.0).astype(out_ref.dtype)
        for q, h in enumerate(heads):
            out_ref[0, :, h : h + HEAD_DIM] = result[q * positions : (q + 1) * positions]


def halves(x):
    high = x.astype(jnp.bfloat16)
    return high, (x - high.astype(jnp.float32)).astype(jnp.bfloat16)


def within_kernel(
    rate_ref, skip_ref, spread_ref, step_ref, read_ref, write_ref, input_ref, gate_ref, fixed_ref, scaled_ref
):
    positions = input_ref.shape[1]
    heads = step_ref.shape[2]
    step = step_ref[0]
    later = lax.broadcasted_iota(jnp.int32, (positions, positions), 0)
    earlier = lax.broadcasted_iota(jnp.int32, (positions, positions), 1)
    causal = earlier <= later
    decays = step * (-jnp.exp(rate_ref[...]))
    running = lax.dot_general(
        causal.astype(jnp.float32),
        decays,
        (((1,), (0,)), ((), ())),
        precision=lax.Precision.HIGHEST,
        preferred_element_type=jnp.float32,
    )
    decay = jnp.exp(running)
    growth = jnp.exp(-running) * step
    both = jnp.concatenate([decay, growth], axis=0)
    high, low = halves(both)
    wide = jnp.dot(
        jnp.concatenate([high, low], axis=1), spread_ref[...], preferred_element_type=jnp.float32
    )
    decay, growth = wide[:positions], wide[positions:]
    contact = lax.dot_general(
        read_ref[0], write_ref[0], (((1,), (1,)), ((), ())), preferred_element_type=jnp.float32
    )
    contact = jnp.where(causal, contact, 0.0)
    contact_high, contact_low = halves(contact)
    inputs = input_ref[0].astype(jnp.float32)
    weighed = (inputs * growth).astype(jnp.bfloat16)
    within = jnp.dot(
        jnp.concatenate([contact_high, contact_low], axis=1),
        jnp.concatenate([weighed, weighed], axis=0),
        preferred_element_type=jnp.float32,
    )
    gate = gate_ref[0].astype(jnp.float32)
    gate = gate / (1.0 + jnp.exp(-gate))
    fixed_ref[0] = gate * (decay * within + skip_ref[...] * inputs)
    scaled_ref[0] = gate * decay


def finish_kernel(
    replicas, slots, members, chained, plan_ref, live_ref, gain_ref, fixed_ref, scaled_ref, *rest
):
    count = live_ref.shape[0]
    _, at_source, at_rank, at_order, at_ends, _ = places(replicas, slots, count)
    arrived = dict(zip(members, rest[: len(members)]))
    out_ref, ready, sem = rest[len(members) + chained :]
    positions, channels = fixed_ref.shape[1:]
    first = plan_ref[at_ends + members[0] - 1] if members[0] else 0
    last = plan_ref[at_ends + members[-1]]

    def copy(i):
        request = plan_ref[at_order + i]
        return pltpu.make_async_copy(ready.at[request], out_ref.at[request], sem)

    def finish(i, carry):
        request = plan_ref[at_order + i]
        alive = lax.broadcasted_iota(jnp.int32, (positions, 1), 0) < live_ref[request]
        for known in members:

            @pl.when(plan_ref[at_source + request] == known)
            def _(known=known):
                carried = arrived[known][plan_ref[at_rank + request]].astype(jnp.float32)
                gated = fixed_ref[request] + scaled_ref[request] * carried
                square = jnp.sum(gated * gated, axis=1, keepdims=True) * (1.0 / channels)
                factor = jnp.where(alive, lax.rsqrt(square + 1e-05), 0.0)
                ready[request] = (gated * factor * gain_ref[...]).astype(out_ref.dtype)

        copy(i).start()
        return carry

    lax.fori_loop(first, last, finish, 0)

    def wait(i, carry):
        copy(i).wait()
        return carry

    lax.fori_loop(first, last, wait, 0)


def per_device(
    holder,
    cache_slot,
    prefix_pages,
    page_ids,
    suffix_length,
    cache_states,
    page_keys,
    page_values,
    ssm_inputs,
    step_sizes,
    log_rates,
    write_map,
    read_map,
    skip_gain,
    gate_values,
    norm_gain,
    queries,
    suffix_keys,
    suffix_values,
):
    replicas = lax.axis_size("replica")
    assert replicas & (replicas - 1) == 0
    myself = lax.axis_index("replica").astype(jnp.int32)
    count, positions, channels = ssm_inputs.shape
    slots = (count + replicas - 1) // replicas
    heads = log_rates.shape[0]
    width = channels // heads
    assert write_map.shape[2] == STATE
    page_len, row_width = page_keys.shape[1:]
    most = page_ids.shape[1]
    kv_here = row_width // HEAD_DIM
    per_kv = queries.shape[2] // row_width
    bf16, f32 = jnp.bfloat16, jnp.float32
    steps = partner_steps(replicas)
    shape = jax.ShapeDtypeStruct

    me = myself.reshape(1)
    holder_row = holder.T
    page_rows = page_ids.T
    def exchange(x, step):
        return lax.ppermute(x, "replica", [(i, i ^ step) for i in range(replicas)])

    at_state, at_source, at_rank, at_order, at_ends, at_me = places(replicas, slots, count)
    third = max(1, (replicas - 1) // 3)
    far, near = steps[:third], steps[third:]
    page_shape = shape((slots, 2, most * page_len, row_width), bf16)
    first = pl.pallas_call(
        functools.partial(first_kernel, replicas, slots, count, most, page_len, far),
        out_shape=[page_shape] * len(far) + [shape((slots, positions, STATE), bf16)] * (replicas - 1),
        in_specs=[SMEM] * 3 + [ANY] * 3,
        out_specs=[ANY] * (len(far) + replicas - 1),
        scratch_shapes=[
            pltpu.VMEM(page_keys.shape, bf16),
            pltpu.VMEM(page_values.shape, bf16),
            pltpu.VMEM((len(far), *page_shape.shape), bf16),
            pltpu.SMEM((replicas,), jnp.int32),
            pltpu.VMEM(read_map.shape, bf16),
            pltpu.SemaphoreType.DMA((4,)),
            pltpu.SemaphoreType.DMA((len(far),)),
        ],
        compiler_params=WIDE,
        name="first",
    )(me, holder_row, page_rows, page_keys, page_values, read_map)
    pages = {s: exchange(x, s) for s, x in zip(far, first)}
    reads = {s: exchange(x, s) for s, x in zip(steps, first[len(far) :])}
    waited = []
    second = pl.pallas_call(
        functools.partial(second_kernel, replicas, slots, count, most, page_len, near, len(waited)),
        out_shape=[page_shape] * len(near) + [shape((at_me + 1,), jnp.int32)],
        in_specs=[SMEM] * 4 + [ANY] * (2 + len(waited)),
        out_specs=[ANY] * len(near) + [SMEM],
        scratch_shapes=[
            pltpu.VMEM(page_keys.shape, bf16),
            pltpu.VMEM(page_values.shape, bf16),
            pltpu.VMEM((len(near), *page_shape.shape), bf16),
            pltpu.SMEM((replicas,), jnp.int32),
            pltpu.SemaphoreType.DMA((2,)),
            pltpu.SemaphoreType.DMA((len(near),)),
        ],
        compiler_params=WIDE,
        name="second",
    )(me, holder_row, cache_slot, page_rows, page_keys, page_values, *waited)
    pages.update({s: exchange(x, s) for s, x in zip(near, second[:-1])})
    reads[0] = read_map
    plan = second[-1]

    states = cache_states.reshape(cache_states.shape[0], channels, STATE)
    carried = {}
    token = []
    half = max(1, replicas // 2)
    for served in (steps + [0],):
        results = pl.pallas_call(
            functools.partial(carried_kernel, replicas, slots, count, served),
            out_shape=[shape((slots, positions, channels), bf16)] * len(served),
            grid_spec=pltpu.PrefetchScalarGridSpec(
                num_scalar_prefetch=1,
                grid=(1,),
                in_specs=[ANY] * (len(served) + 1 + len(token)),
                out_specs=[pl.BlockSpec((slots, positions, channels), lambda i, plan: (0, 0, 0))] * len(served),
                scratch_shapes=[
                    pltpu.VMEM((len(served), slots, positions, STATE), bf16),
                    pltpu.VMEM((len(served), channels, slots * STATE), bf16),
                    pltpu.SemaphoreType.DMA((len(served), 2 * slots)),
                ],
            ),
            compiler_params=WIDE,
            cost_estimate=pl.CostEstimate(
                flops=64 * len(served) * slots * positions * channels * STATE,
                bytes_accessed=2 * len(served) * slots * channels * (STATE + positions),
                transcendentals=0,
            ),
            name="carried",
        )(plan, *[reads[s] for s in served], states, *token)
        token = [results[0]]
        for s, x in zip(served, results):
            carried[s] = exchange(x, s) if s else x

    spread = (jnp.arange(2 * heads)[:, None] % heads == jnp.arange(channels)[None, :] // width).astype(bf16)
    skip_wide = jnp.repeat(skip_gain, width).reshape(1, channels)
    row = lambda i: (i, 0, 0)
    whole = lambda i: (0, 0)
    fixed, scaled = pl.pallas_call(
        within_kernel,
        out_shape=[shape((count, positions, channels), f32)] * 2,
        grid=(count,),
        in_specs=[
            pl.BlockSpec((1, heads), whole),
            pl.BlockSpec((1, channels), whole),
            pl.BlockSpec((2 * heads, channels), whole),
            pl.BlockSpec((1, positions, heads), row),
            pl.BlockSpec((1, positions, STATE), row),
            pl.BlockSpec((1, positions, STATE), row),
            pl.BlockSpec((1, positions, channels), row),
            pl.BlockSpec((1, positions, channels), row),
        ],
        out_specs=[pl.BlockSpec((1, positions, channels), row)] * 2,
        cost_estimate=pl.CostEstimate(
            flops=2 * count * positions * channels * positions * 8,
            bytes_accessed=count * positions * channels * 12,
            transcendentals=count * positions * channels,
        ),
        compiler_params=PARAMS,
        name="within",
    )(
        log_rates.reshape(1, heads),
        skip_wide,
        spread,
        step_sizes,
        read_map,
        write_map,
        ssm_inputs,
        gate_values,
    )

    row5 = lambda i, *refs: (i, 0, 0)
    attention_output = pl.pallas_call(
        functools.partial(attention_kernel, replicas, kv_here, per_kv, page_len, most, slots),
        out_shape=shape((count, positions, queries.shape[2]), bf16),
        grid_spec=pltpu.PrefetchScalarGridSpec(
            num_scalar_prefetch=4,
            grid=(count,),
            in_specs=[
                pl.BlockSpec((1, positions, queries.shape[2]), row5),
                pl.BlockSpec((1, positions, row_width), row5),
                pl.BlockSpec((1, positions, row_width), row5),
            ]
            + [ANY] * (replicas + 1),
            out_specs=pl.BlockSpec((1, positions, queries.shape[2]), row5),
            scratch_shapes=[
                pltpu.VMEM((2, 2, most * page_len, row_width), bf16),
                pltpu.SemaphoreType.DMA((2,)),
            ],
        ),
        cost_estimate=pl.CostEstimate(
            flops=4 * count * positions * queries.shape[2] * (most * page_len + positions),
            bytes_accessed=count * (positions * queries.shape[2] * 4 + most * page_len * row_width * 4),
            transcendentals=count * positions * kv_here * per_kv * (most * page_len + positions),
        ),
        compiler_params=PARAMS,
        name="attention",
    )(
        plan,
        prefix_pages,
        suffix_length,
        page_rows,
        queries,
        suffix_keys,
        suffix_values,
        *[pages[s] for s in steps],
        page_keys,
        page_values,
    )

    mamba_output = None
    for members in (list(range(half)), list(range(half, replicas))):
        chained = 0 if mamba_output is None else 1
        mamba_output = pl.pallas_call(
            functools.partial(finish_kernel, replicas, slots, members, chained),
            out_shape=shape((count, positions, channels), bf16),
            in_specs=[SMEM] * 2 + [VMEM] * (3 + len(members)) + [ANY] * chained,
            out_specs=ANY,
            scratch_shapes=[pltpu.VMEM((count, positions, channels), bf16), pltpu.SemaphoreType.DMA],
            input_output_aliases={5 + len(members): 0} if chained else {},
            compiler_params=PARAMS,
            cost_estimate=pl.CostEstimate(
                flops=len(members) * slots * positions * channels * 8,
                bytes_accessed=len(members) * slots * positions * channels * 12,
                transcendentals=0,
            ),
            name="finish",
        )(
            plan,
            suffix_length,
            norm_gain.reshape(1, channels),
            fixed,
            scaled,
            *[carried[s] for s in members],
            *([mamba_output] if chained else []),
        )
    return (mamba_output, attention_output)


def solution(mesh):
    return jax.shard_map(
        per_device,
        mesh=mesh,
        in_specs=(
            P("groups", None),
            P("groups"),
            P(("groups", "replica")),
            P("groups", None),
            P(("groups", "replica")),
            P(("groups", "replica"), "tensor", None, None),
            P(("groups", "replica"), None, "tensor"),
            P(("groups", "replica"), None, "tensor"),
            P(("groups", "replica"), None, "tensor"),
            P(("groups", "replica"), None, "tensor"),
            P("tensor"),
            P(("groups", "replica"), None, "tensor"),
            P(("groups", "replica"), None, "tensor"),
            P("tensor"),
            P(("groups", "replica"), None, "tensor"),
            P("tensor"),
            P(("groups", "replica"), None, "tensor"),
            P(("groups", "replica"), None, "tensor"),
            P(("groups", "replica"), None, "tensor"),
        ),
        out_specs=(
            P(("groups", "replica"), None, "tensor"),
            P(("groups", "replica"), None, "tensor"),
        ),
        check_vma=False,
    )
```
